256 devices in a mesh: pop: 32 (over y, z_lo, core), tp: 8 (over z_hi, x).
Axes of the slice: x: 4, y: 4, z: 8 (z_hi: 2, z_lo: 4; z = z_hi * 4 + z_lo), core: 2. Of those that a mesh axis runs over, the one named last changes fastest.
Arguments:
- gate_left: bfloat16 [256, 4, 8192], P(('pop', 'tp')), may hold values from -6 to 6
- up_left: bfloat16 [256, 4, 8192], P(('pop', 'tp')), may hold values from -6 to 6
- gate_right: bfloat16 [256, 4, 28672], P('pop', None, 'tp'), may hold values from -6 to 6
- up_right: bfloat16 [256, 4, 28672], P('pop', None, 'tp'), may hold values from -6 to 6
- fitness_order: int32 [256], P(('pop', 'tp')), may hold values from 0 to 255, each once
- member_scale: float32 [256], P(('pop', 'tp')), may hold values from 0.5 to 2
Outputs:
- gate_grad: bfloat16 [8192, 28672], P('pop', 'tp')
- up_grad: bfloat16 [8192, 28672], P('pop', 'tp')
The draws below stay inside these ranges and needn't reach their ends.
Inputs may be any that keep to these rules, and one draw needn't show every extreme that they name: `fitness_order`: each of 0 to 255 appears once.
All inputs are finite; a program needn't handle non-finite values.
Results may differ from the reference program's by a relative error of at most 0.0049.
Values may be sent and summed in bfloat16 or wider, within the bound.
No kernel may reach another device: no remote copies, remote signals or barrier semaphores. Data moves between devices by JAX's collectives and lax.ppermute only.
A program may use at most 128 MiB of HBM per device.

```python
import math
import jax
import jax.numpy as jnp
from jax import lax

D = 8192
FF = 28672
R = 4
MEMBERS = 256


def block_scale(key, dims, shards, least, high):
    loudness, own = 1.0, jax.random.fold_in(key, 6)
    for axis_at, parts in shards:
        steps = jnp.exp(jax.random.uniform(jax.random.fold_in(own, axis_at), (parts,), jnp.float32, least / len(shards), high / len(shards)))
        loudness = loudness * jnp.repeat(steps, dims[axis_at] // parts).reshape([-1 if axis == axis_at else 1 for axis in range(len(dims))])
    return loudness


def bell_draw(key, extent, deviation, bound, pieces=(), kind=jnp.bfloat16):
    level = block_scale(key, extent, pieces, -0.22, 0.18) if pieces else 1.0
    array = jax.random.normal(key, extent, jnp.float32) * deviation * level
    return jnp.minimum(jnp.maximum(array, -bound), bound).astype(kind)


def setup_inputs(seed: int = 0) -> dict:
    splits = jax.random.split(jax.random.key(seed), 7)
    gate_left = bell_draw(splits[0], (MEMBERS, R, D), 1.0, 6.0, ((0, 256),))
    up_left = bell_draw(splits[1], (MEMBERS, R, D), 1.0, 6.0, ((0, 256),))
    gate_right = bell_draw(splits[2], (MEMBERS, R, FF), 1.0, 6.0, ((0, 32), (2, 8)))
    up_right = bell_draw(splits[3], (MEMBERS, R, FF), 1.0, 6.0, ((0, 32), (2, 8)))
    fitness_order = jax.random.permutation(splits[4], MEMBERS).astype(jnp.int32)
    member_scale = jnp.clip(jnp.exp(math.log(2.0) - 1.3862944 * jax.random.uniform(splits[5], (MEMBERS,), jnp.float32) ** block_scale(splits[5], (MEMBERS,), ((0, 256),), -0.2, 0.2)), 0.5, 2.0)
    return {"gate_left": gate_left, "up_left": up_left, "gate_right": gate_right, "up_right": up_right, "fitness_order": fitness_order, "member_scale": member_scale}


def weigh(left, coef):
    return (coef[:, None, None] * left.astype(jnp.float32)).astype(jnp.bfloat16)

def contract(left, right):
    return lax.dot_general(left, right, (((0, 1), (0, 1)), ((), ())), preferred_element_type=jnp.float32)

def reference(gate_left, up_left, gate_right, up_right, fitness_order, member_scale):
    centered = (2 * fitness_order - (MEMBERS - 1)).astype(jnp.float32)
    coef = centered * member_scale / ((MEMBERS - 1) * math.sqrt(MEMBERS * R))
    gate_weighted = weigh(gate_left, coef)
    up_weighted = weigh(up_left, coef)
    gate_grad = contract(gate_weighted, gate_right).astype(jnp.bfloat16)
    up_grad = contract(up_weighted, up_right).astype(jnp.bfloat16)
    return (gate_grad, up_grad)
```

```python
import functools
import math

import jax
import jax.numpy as jnp
from jax import lax
from jax.experimental import pallas as pl
from jax.experimental.pallas import tpu as pltpu
from jax.sharding import Mesh, PartitionSpec as P

Y, Z, C, H, X = 4, 4, 2, 2, 4
FIRST = 512


def shift(x, axis, by):
    n = lax.axis_size(axis)
    return lax.ppermute(x, axis, [(i, (i + by) % n) for i in range(n)])


def spread(x):
    half = x.shape[0] // 2
    up, down = shift(x, "y", 1), shift(x, "y", -1)
    return up, down, shift(up[:half], "y", 1), shift(down[half:], "y", -1)


def left_kernel(place_ref, left_ref, out_ref):
    y, z = place_ref[0], place_ref[1]
    for d in range(Z):
        parts = []
        for j in (0, 1, Y - 1, 2):
            chip = lax.rem(y + Y - j, Y) * Z + lax.rem(z + Z - d, Z)
            parts += [left_ref[x, h, chip].astype(jnp.float32) for h in range(H) for x in range(X)]
        out_ref[d] = jnp.concatenate(parts, axis=0).T.astype(out_ref.dtype)


def arrange_left(place, left):
    rows = left.shape[-1]
    depth = Y * H * X * left.shape[3]
    return pl.pallas_call(
        left_kernel,
        out_shape=jax.ShapeDtypeStruct((Z, rows, depth), left.dtype),
        in_specs=[pl.BlockSpec(memory_space=pltpu.SMEM), pl.BlockSpec(memory_space=pltpu.VMEM)],
        out_specs=pl.BlockSpec(memory_space=pltpu.VMEM),
        name="arrange_left",
    )(place, left)


def mul_kernel(groups, width, core_ref, left_ref, *refs):
    pieces, (keep_ref, send_ref) = refs[:-2], refs[-2:]
    rows = keep_ref.shape[0]
    mine = pl.multiple_of(core_ref[0] * rows, rows)
    other = pl.multiple_of((1 - core_ref[0]) * rows, rows)

    def step(i, _):
        at = pl.multiple_of(i * width, width)
        keep = jnp.zeros((rows, width), jnp.float32)
        send = jnp.zeros((rows, width), jnp.float32)
        for d, group in enumerate(groups):
            part = []
            for piece, row, count, offset in group:
                part.append(pieces[piece][pl.ds(row, count), pl.ds(pl.multiple_of(at + offset, 128), width)])
            right = jnp.concatenate(part, axis=0)
            keep += jnp.dot(left_ref[d, pl.ds(mine, rows)], right, preferred_element_type=jnp.float32)
            send += jnp.dot(left_ref[d, pl.ds(other, rows)], right, preferred_element_type=jnp.float32)
        keep_ref[:, pl.ds(at, width)] = keep.astype(keep_ref.dtype)
        send_ref[:, pl.ds(at, width)] = send.astype(send_ref.dtype)
        return _

    lax.fori_loop(0, keep_ref.shape[1] // width, step, None)


def multiply(core, left, pieces, groups, columns, name):
    rows = left.shape[1] // 2
    shape = jax.ShapeDtypeStruct((rows, columns), left.dtype)
    vmem = pl.BlockSpec(memory_space=pltpu.VMEM)
    return pl.pallas_call(
        functools.partial(mul_kernel, groups, 256),
        out_shape=(shape, shape),
        in_specs=[pl.BlockSpec(memory_space=pltpu.SMEM)] + [vmem] * (1 + len(pieces)),
        out_specs=(vmem, vmem),
        compiler_params=pltpu.CompilerParams(vmem_limit_bytes=24 << 20),
        name=name,
    )(core, left, *pieces)


def join_kernel(core_ref, keep_a, keep_b, got_a, got_b, gate_ref, up_ref, sems):
    cut = keep_a.shape[1]

    def put(gate, up):
        copies = []
        for out, (a, b) in ((gate_ref, gate), (up_ref, up)):
            copies.append(pltpu.make_async_copy(a, out.at[:, pl.ds(0, cut)], sems.at[len(copies)]))
            copies.append(pltpu.make_async_copy(b, out.at[:, pl.ds(cut, b.shape[1])], sems.at[len(copies)]))
        for copy in copies:
            copy.start()
        for copy in copies:
            copy.wait()

    @pl.when(core_ref[0] == 0)
    def _():
        put((keep_a, keep_b), (got_a, got_b))

    @pl.when(core_ref[0] == 1)
    def _():
        put((got_a, got_b), (keep_a, keep_b))


def join(core, keep_a, keep_b, got_a, got_b):
    rows, columns = keep_a.shape[0], keep_a.shape[1] + keep_b.shape[1]
    shape = jax.ShapeDtypeStruct((rows, columns), keep_a.dtype)
    anywhere = pl.BlockSpec(memory_space=pl.ANY)
    return pl.pallas_call(
        join_kernel,
        out_shape=(shape, shape),
        in_specs=[pl.BlockSpec(memory_space=pltpu.SMEM)] + [anywhere] * 4,
        out_specs=(anywhere, anywhere),
        scratch_shapes=[pltpu.SemaphoreType.DMA((4,))],
        compiler_params=pltpu.CompilerParams(vmem_limit_bytes=16 << 20),
        name="join",
    )(core, keep_a, keep_b, got_a, got_b)


def weigh(left, coef):
    return (coef[:, None, None] * left.astype(jnp.float32)).astype(jnp.bfloat16)


def shards(gate_left, up_left, gate_right, up_right, fitness_order, member_scale):
    core = lax.axis_index("c")
    first = core == 0
    place = jnp.stack([lax.axis_index("y"), lax.axis_index("z")]).astype(jnp.int32)
    core_at = core.reshape(1).astype(jnp.int32)
    total = Y * Z * C * H * X
    rank, columns = gate_right.shape[1:]

    mine = jnp.where(first, gate_right, up_right)
    got = shift(jnp.where(first, up_right, gate_right), "c", 1)
    own = jnp.concatenate([jnp.where(first, mine, got), jnp.where(first, got, mine)], axis=1)
    own = own.reshape(-1, columns)

    centered = (2 * fitness_order - (total - 1)).astype(jnp.float32)
    coef = centered * member_scale / ((total - 1) * math.sqrt(total * rank))
    gate_w, up_w = weigh(gate_left, coef)[0], weigh(up_left, coef)[0]
    left_mine = jnp.where(first, gate_w, up_w)
    left_got = shift(jnp.where(first, up_w, gate_w), "c", 1)
    left = jnp.concatenate([jnp.where(first, left_mine, left_got), jnp.where(first, left_got, left_mine)], axis=0)
    left = left.reshape(C * rank, Y * Z, -1).transpose(1, 0, 2)
    left = jnp.concatenate([left, left], axis=0)
    left = lax.all_to_all(left, ("h", "y", "z"), split_axis=0, concat_axis=0, tiled=True)
    left = lax.all_gather(left, "x", axis=0, tiled=False)
    left = left.reshape(X, H, Y * Z, C * rank, -1)
    left = arrange_left(place, left)

    n = own.shape[0]
    half = n // 2
    y0 = spread(own)
    z1 = shift(own[:, FIRST:], "z", 1)
    z2 = shift(z1, "z", 1)
    z3 = shift(z2, "z", 1)
    y1 = spread(z1)
    z23 = jnp.concatenate([z2[:half], z3[:half], z2[half:], z3[half:]], axis=0)
    y23 = spread(z23)
    a0 = jnp.concatenate([own[:, :FIRST]] + [part[:, :FIRST] for part in y0], axis=0)
    a1 = shift(a0, "z", 1)
    a2 = shift(a1, "z", 1)
    a3 = shift(a2, "z", 1)

    a_groups = [[(d, 0, Y * n, 0)] for d in range(Z)]
    keep_a, send_a = multiply(core_at, left, [a0, a1, a2, a3], a_groups, FIRST, "multiply_a")
    got_a = shift(send_a, "c", 1)
    pieces = [own, *y0, z1, *y1, z23, *y23]
    b_groups = [
        [(0, 0, n, FIRST), (1, 0, n, FIRST), (2, 0, n, FIRST), (3, 0, half, FIRST), (4, 0, half, FIRST)],
        [(5, 0, n, 0), (6, 0, n, 0), (7, 0, n, 0), (8, 0, half, 0), (9, 0, half, 0)],
    ]
    for k in (0, 1):
        low, high = k * half, (k + 2) * half
        group = []
        for piece in (10, 11, 12):
            group += [(piece, low, half, 0), (piece, high, half, 0)]
        group += [(13, low, half, 0), (14, low, half, 0)]
        b_groups.append(group)
    keep_b, send_b = multiply(core_at, left, pieces, b_groups, columns - FIRST, "multiply_b")
    got_b = shift(send_b, "c", 1)
    return tuple(join(core_at, keep_a, keep_b, got_a, got_b))


def solution(mesh):
    fine = Mesh(mesh.devices.reshape(Y, Z, C, H, X), ("y", "z", "c", "h", "x"))
    pop, tp = ("y", "z", "c"), ("h", "x")
    in_specs = (
        P(pop + tp, None, None),
        P(pop + tp, None, None),
        P(pop, None, tp),
        P(pop, None, tp),
        P(pop + tp),
        P(pop + tp),
    )
    out_specs = (P(pop, tp), P(pop, tp))
    return jax.shard_map(shards, mesh=fine, in_specs=in_specs, out_specs=out_specs, check_vma=False)
```

```python
import functools
import math

import jax
import jax.numpy as jnp
from jax import lax
from jax.experimental import pallas as pl
from jax.experimental.pallas import tpu as pltpu
from jax.sharding import Mesh, PartitionSpec as P

Y, Z, C, H, X = 4, 4, 2, 2, 4
FIRST = 0


def shift(x, axis, by):
    n = lax.axis_size(axis)
    return lax.ppermute(x, axis, [(i, (i + by) % n) for i in range(n)])


def left_kernel(place_ref, *refs):
    *left_refs, first_ref, second_ref, last_ref, held = refs
    x, y, z, h = place_ref[0], place_ref[1], place_ref[2], place_ref[3]
    for r, left_ref in enumerate(left_refs):
        held[r] = left_ref[...].astype(held.dtype)
    size = H * X * held.shape[3]
    for d in range(Z):
        parts = []
        for from_y in (0, 1, Y - 1, 2):
            chip = lax.rem(y + Y - from_y, Y) * Z + lax.rem(z + Z - d, Z)
            for at_h in range(H):
                for at_x in range(X):
                    parts.append(held[lax.rem(x + X - at_x, X), lax.rem(h + at_h, H), chip])
        block = jnp.concatenate(parts, axis=0).T.astype(first_ref.dtype)
        if d < Z // 2:
            first_ref[:, d * Y * size : (d + 1) * Y * size] = block
        elif d < Z - 1:
            second_ref[:, (d - Z // 2) * Y * size : (d - Z // 2 + 1) * Y * size] = block
        else:
            second_ref[:, (d - Z // 2) * Y * size :] = block[:, : (Y - 1) * size]
            last_ref[...] = block[:, (Y - 1) * size :]


def arrange_left(place, lefts):
    rows = lefts[0].shape[-1]
    size = H * X * lefts[0].shape[2]
    vmem = pl.BlockSpec(memory_space=pltpu.VMEM)
    return pl.pallas_call(
        left_kernel,
        out_shape=(
            jax.ShapeDtypeStruct((rows, Y * Z * size // 2), lefts[0].dtype),
            jax.ShapeDtypeStruct((rows, (Y * Z // 2 - 1) * size), lefts[0].dtype),
            jax.ShapeDtypeStruct((rows, size), lefts[0].dtype),
        ),
        in_specs=[pl.BlockSpec(memory_space=pltpu.SMEM)] + [vmem] * X,
        out_specs=(vmem, vmem, vmem),
        scratch_shapes=[pltpu.VMEM((X,) + lefts[0].shape, jnp.float32)],
        compiler_params=pltpu.CompilerParams(vmem_limit_bytes=8 << 20),
        cost_estimate=pl.CostEstimate(flops=0, bytes_accessed=6 << 20, transcendentals=0),
        name="arrange_left",
    )(place, *lefts)


def part_kernel(ranges, width, left_ref, *refs):
    *arrays, out_ref, held, sems = refs
    total_ref = arrays.pop() if len(arrays) > len({which for which, _, _ in ranges}) else None
    columns = out_ref.shape[1]
    cuts = (0, columns // (2 * width) * width, columns)

    def copies(side):
        found, at = [], 0
        part = pl.ds(cuts[side], cuts[side + 1] - cuts[side])
        for which, row, count in ranges:
            source, target = arrays[which].at[pl.ds(row, count), part], held.at[pl.ds(at, count), part]
            found.append(pltpu.make_async_copy(source, target, sems.at[side, len(found)]))
            at += count
        return found

    for side in (0, 1):
        for copy in copies(side):
            copy.start()
    for side in (0, 1):
        for copy in copies(side):
            copy.wait()

        def step(i, _):
            at = pl.ds(pl.multiple_of(i * width, width), width)
            product = jnp.dot(left_ref[...], held[:, at], preferred_element_type=jnp.float32)
            out_ref[:, at] = product if total_ref is None else total_ref[:, at] + product
            return _

        lax.fori_loop(cuts[side] // width, cuts[side + 1] // width, step, None)


def multiply_part(left, pieces, total, name):
    arrays, ranges = [], []
    for array, row, count in pieces:
        known = [k for k, other in enumerate(arrays) if other is array]
        if not known:
            arrays.append(array)
        ranges.append((known[0] if known else len(arrays) - 1, row, count))
    rows, depth = left.shape
    columns = arrays[0].shape[1]
    vmem = pl.BlockSpec(memory_space=pltpu.VMEM)
    totals = [] if total is None else [total]
    return pl.pallas_call(
        functools.partial(part_kernel, ranges, 256),
        out_shape=jax.ShapeDtypeStruct((rows, columns), jnp.float32),
        in_specs=[vmem] + [pl.BlockSpec(memory_space=pl.ANY)] * len(arrays) + [vmem] * len(totals),
        out_specs=vmem,
        scratch_shapes=[
            pltpu.VMEM((depth, columns), left.dtype),
            pltpu.SemaphoreType.DMA((2, len(ranges))),
        ],
        input_output_aliases={1 + len(arrays): 0} if totals else {},
        compiler_params=pltpu.CompilerParams(vmem_limit_bytes=24 << 20),
        cost_estimate=pl.CostEstimate(
            flops=4 * rows * columns * depth, bytes_accessed=12 << 20, transcendentals=0
        ),
        name=name,
    )(left, *arrays, *totals)


def last_kernel(cut, width, core_ref, left_ref, total_ref, *refs):
    *right_refs, keep_ref, send_ref = refs
    rows, columns = keep_ref.shape
    mine = pl.multiple_of(core_ref[0] * rows, rows)
    other = pl.multiple_of((1 - core_ref[0]) * rows, rows)

    def step(i, _):
        at = pl.ds(pl.multiple_of(i * width, width), width)
        from_at = pl.ds(pl.multiple_of(cut + i * width, width), width)
        right = jnp.concatenate([ref[:, from_at] for ref in right_refs], axis=0)
        for out_ref, row in ((send_ref, other), (keep_ref, mine)):
            total = total_ref[pl.ds(row, rows), from_at]
            total += jnp.dot(left_ref[pl.ds(row, rows)], right, preferred_element_type=jnp.float32)
            out_ref[:, at] = total.astype(out_ref.dtype)
        return _

    lax.fori_loop(0, columns // width, step, None)


def multiply_last(core, left, total, last, cut, end, name):
    rows, columns = total.shape[0] // 2, end - cut
    shape = jax.ShapeDtypeStruct((rows, columns), left.dtype)
    vmem = pl.BlockSpec(memory_space=pltpu.VMEM)
    return pl.pallas_call(
        functools.partial(last_kernel, cut, 256),
        out_shape=(shape, shape),
        in_specs=[pl.BlockSpec(memory_space=pltpu.SMEM)] + [vmem] * (2 + len(last)),
        out_specs=(vmem, vmem),
        compiler_params=pltpu.CompilerParams(vmem_limit_bytes=14 << 20),
        cost_estimate=pl.CostEstimate(flops=1024 * rows * columns, bytes_accessed=6 << 20, transcendentals=0),
        name=name,
    )(core, left, total, *last)


def join_kernel(core_ref, keep_0, keep_1, got_0, got_1, gate_ref, up_ref, sems):
    def put(gate, up):
        copies = []
        for out, halves in ((gate_ref, gate), (up_ref, up)):
            for half, at in zip(halves, (0, halves[0].shape[1])):
                to = out.at[:, pl.ds(at, half.shape[1])]
                copies.append(pltpu.make_async_copy(half, to, sems.at[len(copies)]))
        for copy in copies:
            copy.start()
        for copy in copies:
            copy.wait()

    @pl.when(core_ref[0] == 0)
    def _():
        put((keep_0, keep_1), (got_0, got_1))

    @pl.when(core_ref[0] == 1)
    def _():
        put((got_0, got_1), (keep_0, keep_1))


def join(core, *halves):
    rows, columns = halves[0].shape[0], halves[0].shape[1] + halves[1].shape[1]
    shape = jax.ShapeDtypeStruct((rows, columns), halves[0].dtype)
    anywhere = pl.BlockSpec(memory_space=pl.ANY)
    return pl.pallas_call(
        join_kernel,
        out_shape=(shape, shape),
        in_specs=[pl.BlockSpec(memory_space=pltpu.SMEM)] + [anywhere] * 4,
        out_specs=(anywhere, anywhere),
        scratch_shapes=[pltpu.SemaphoreType.DMA((4,))],
        compiler_params=pltpu.CompilerParams(vmem_limit_bytes=4 << 20),
        name="join",
    )(core, *halves)


def weigh(left, coef):
    return (coef[:, None, None] * left.astype(jnp.float32)).astype(jnp.bfloat16)


def shards(gate_left, up_left, gate_right, up_right, fitness_order, member_scale):
    y, z, core = lax.axis_index("y"), lax.axis_index("z"), lax.axis_index("c")
    first = core == 0
    place = jnp.stack([lax.axis_index("x"), y, z, lax.axis_index("h")]).astype(jnp.int32)
    token = core.reshape(1).astype(jnp.int32)
    total = Y * Z * C * H * X
    rank, columns = gate_right.shape[1:]

    def event(*arrived):
        nonlocal token
        *arrived, token = lax.optimization_barrier((*arrived, token))
        return arrived

    gate_got, up_got = shift(gate_right, "c", 1), shift(up_right, "c", 1)
    own = jnp.concatenate([jnp.where(first, gate_right, up_got), jnp.where(first, gate_got, up_right)], axis=1)
    own = own.reshape(-1, columns)

    centered = (2 * fitness_order - (total - 1)).astype(jnp.float32)
    coef = centered * member_scale / ((total - 1) * math.sqrt(total * rank))
    gate_w, up_w = weigh(gate_left, coef)[0], weigh(up_left, coef)[0]
    left_mine = jnp.where(first, gate_w, up_w)
    left_got = shift(jnp.where(first, up_w, gate_w), "c", 1)
    left = jnp.concatenate([jnp.where(first, left_mine, left_got), jnp.where(first, left_got, left_mine)], axis=0)

    def deal(block, axis, at, size):
        width = block.shape[-1] // size
        parts = []
        for by in range(size):
            start = lax.rem(at + by, size) * width
            part = lax.dynamic_slice_in_dim(block, start, width, axis=block.ndim - 1)
            parts.append(shift(part, axis, by) if by else part)
        return parts

    n = own.shape[0]
    half = n // 2

    def both(block, up=None, down=None):
        if up is None:
            return shift(block, "y", 1), shift(block, "y", -1)
        up = jnp.concatenate([block, up[:half]], axis=0)
        down = jnp.concatenate([block, down[half:n]], axis=0)
        return shift(up, "y", 1), shift(down, "y", -1)

    left = left.reshape(C * rank, Y * Z, -1).transpose(1, 0, 2)
    left = lax.all_to_all(left, ("y", "z"), split_axis=0, concat_axis=0, tiled=True)
    own, place = event(own, place)
    up0, down0 = both(own)
    z1 = shift(own, "z", 1)
    up0, down0, z1, left = event(up0, down0, z1, left)

    up1, down1 = both(z1, up0, down0)
    z2 = shift(z1, "z", 1)
    left_h = shift(left, "h", 1)
    up1, down1, z2, left, left_h = event(up1, down1, z2, left, left_h)

    up2, down2 = both(z2, up1, down1)
    z3 = shift(z2, "z", 1)
    left = jnp.stack([left, left_h])
    left_1, left_3 = shift(left, "x", 1), shift(left, "x", 3)
    up2, down2, z3, left, left_1, left_3 = event(up2, down2, z3, left, left_1, left_3)

    up3, down3 = both(z3, up2, down2)
    left_0, left_1, left_2 = arrange_left(place, [left, left_1, shift(left, "x", 2), left_3])

    def slot(block, up, down, up_next, down_next):
        return [(block, 0, n), (up, 0, n), (down, 0, n), (up_next, n, half), (down_next, n, half)]

    total = multiply_part(left_0, slot(own, up0, down0, up1, down1) + slot(z1, up1, down1, up2, down2), None, "multiply_0")
    up3, down3, total = event(up3, down3, total)

    up4, down4 = shift(up3[:half], "y", 1), shift(down3[half:n], "y", -1)
    pieces = slot(z2, up2, down2, up3, down3) + [(z3, 0, n), (up3, 0, n), (down3, 0, n)]
    total = multiply_part(left_1, pieces, total, "multiply_1")
    up4, down4, total = event(up4, down4, total)
    cut = columns // 2
    keep_0, send_0 = multiply_last(token, left_2, total, [up4, down4], 0, cut, "multiply_2")
    got_0 = shift(send_0, "c", 1)
    keep_1, send_1 = multiply_last(token, left_2, total, [up4, down4], cut, columns, "multiply_3")
    got_1 = shift(send_1, "c", 1)
    return tuple(join(token, keep_0, keep_1, got_0, got_1))


def solution(mesh):
    fine = Mesh(mesh.devices.reshape(Y, Z, C, H, X), ("y", "z", "c", "h", "x"))
    pop, tp = ("y", "z", "c"), ("h", "x")
    in_specs = (
        P(pop + tp, None, None),
        P(pop + tp, None, None),
        P(pop, None, tp),
        P(pop, None, tp),
        P(pop + tp),
        P(pop + tp),
    )
    out_specs = (P(pop, tp), P(pop, tp))
    return jax.shard_map(shards, mesh=fine, in_specs=in_specs, out_specs=out_specs, check_vma=False)
```

```python
import functools
import math

import jax
import jax.numpy as jnp
from jax import lax
from jax.experimental import pallas as pl
from jax.experimental.pallas import tpu as pltpu
from jax.sharding import Mesh, PartitionSpec as P

Y, Z, C, H, X = 4, 4, 2, 2, 4
FIRST = 0


def shift(x, axis, by):
    n = lax.axis_size(axis)
    return lax.ppermute(x, axis, [(i, (i + by) % n) for i in range(n)])


def left_kernel(place_ref, *refs):
    *left_refs, first_ref, second_ref, last_ref, held = refs
    x, y, z, h = place_ref[0], place_ref[1], place_ref[2], place_ref[3]
    for r, left_ref in enumerate(left_refs):
        held[r] = left_ref[...].astype(held.dtype)
    size = H * X * held.shape[3]
    for d in range(Z):
        parts = []
        for from_y in (0, 1, Y - 1, 2):
            chip = lax.rem(y + Y - from_y, Y) * Z + lax.rem(z + Z - d, Z)
            for at_h in range(H):
                for at_x in range(X):
                    parts.append(held[lax.rem(x + X - at_x, X), lax.rem(h + at_h, H), chip])
        block = jnp.concatenate(parts, axis=0).T.astype(first_ref.dtype)
        if d < Z // 2:
            first_ref[:, d * Y * size : (d + 1) * Y * size] = block
        elif d < Z - 1:
            second_ref[:, (d - Z // 2) * Y * size : (d - Z // 2 + 1) * Y * size] = block
        else:
            second_ref[:, (d - Z // 2) * Y * size :] = block[:, : (Y - 1) * size]
            last_ref[...] = block[:, (Y - 1) * size :]


def arrange_left(place, lefts):
    rows = lefts[0].shape[-1]
    size = H * X * lefts[0].shape[2]
    vmem = pl.BlockSpec(memory_space=pltpu.VMEM)
    return pl.pallas_call(
        left_kernel,
        out_shape=(
            jax.ShapeDtypeStruct((rows, Y * Z * size // 2), lefts[0].dtype),
            jax.ShapeDtypeStruct((rows, (Y * Z // 2 - 1) * size), lefts[0].dtype),
            jax.ShapeDtypeStruct((rows, size), lefts[0].dtype),
        ),
        in_specs=[pl.BlockSpec(memory_space=pltpu.SMEM)] + [vmem] * X,
        out_specs=(vmem, vmem, vmem),
        scratch_shapes=[pltpu.VMEM((X,) + lefts[0].shape, jnp.float32)],
        compiler_params=pltpu.CompilerParams(vmem_limit_bytes=8 << 20),
        cost_estimate=pl.CostEstimate(flops=0, bytes_accessed=6 << 20, transcendentals=0),
        name="arrange_left",
    )(place, *lefts)


def part_kernel(ranges, width, left_ref, *refs):
    *arrays, out_ref, held, sems = refs
    total_ref = arrays.pop() if len(arrays) > len({which for which, _, _ in ranges}) else None
    columns = out_ref.shape[1]
    cuts = (0, columns // (2 * width) * width, columns)

    def copies(side):
        found, at = [], 0
        part = pl.ds(cuts[side], cuts[side + 1] - cuts[side])
        for which, row, count in ranges:
            source, target = arrays[which].at[pl.ds(row, count), part], held.at[pl.ds(at, count), part]
            found.append(pltpu.make_async_copy(source, target, sems.at[side, len(found)]))
            at += count
        return found

    for side in (0, 1):
        for copy in copies(side):
            copy.start()
    for side in (0, 1):
        for copy in copies(side):
            copy.wait()

        def step(i, _):
            at = pl.ds(pl.multiple_of(i * width, width), width)
            product = jnp.dot(left_ref[...], held[:, at], preferred_element_type=jnp.float32)
            out_ref[:, at] = product if total_ref is None else total_ref[:, at] + product
            return _

        lax.fori_loop(cuts[side] // width, cuts[side + 1] // width, step, None, unroll=True)


def multiply_part(left, pieces, total, name):
    arrays, ranges = [], []
    for array, row, count in pieces:
        known = [k for k, other in enumerate(arrays) if other is array]
        if not known:
            arrays.append(array)
        ranges.append((known[0] if known else len(arrays) - 1, row, count))
    rows, depth = left.shape
    columns = arrays[0].shape[1]
    vmem = pl.BlockSpec(memory_space=pltpu.VMEM)
    totals = [] if total is None else [total]
    return pl.pallas_call(
        functools.partial(part_kernel, ranges, 256),
        out_shape=jax.ShapeDtypeStruct((rows, columns), jnp.float32),
        in_specs=[vmem] + [pl.BlockSpec(memory_space=pl.ANY)] * len(arrays) + [vmem] * len(totals),
        out_specs=vmem,
        scratch_shapes=[
            pltpu.VMEM((depth, columns), left.dtype),
            pltpu.SemaphoreType.DMA((2, len(ranges))),
        ],
        input_output_aliases={1 + len(arrays): 0} if totals else {},
        compiler_params=pltpu.CompilerParams(vmem_limit_bytes=24 << 20),
        cost_estimate=pl.CostEstimate(
            flops=4 * rows * columns * depth, bytes_accessed=12 << 20, transcendentals=0
        ),
        name=name,
    )(left, *arrays, *totals)


def last_kernel(cut, width, core_ref, left_ref, total_ref, *refs):
    *right_refs, keep_ref, send_ref = refs
    rows, columns = keep_ref.shape
    mine = pl.multiple_of(core_ref[0] * rows, rows)
    other = pl.multiple_of((1 - core_ref[0]) * rows, rows)

    def step(i, _):
        at = pl.ds(pl.multiple_of(i * width, width), width)
        from_at = pl.ds(pl.multiple_of(cut + i * width, width), width)
        right = jnp.concatenate([ref[:, from_at] for ref in right_refs], axis=0)
        for out_ref, row in ((send_ref, other), (keep_ref, mine)):
            total = total_ref[pl.ds(row, rows), from_at]
            total += jnp.dot(left_ref[pl.ds(row, rows)], right, preferred_element_type=jnp.float32)
            out_ref[:, at] = total.astype(out_ref.dtype)
        return _

    lax.fori_loop(0, columns // width, step, None, unroll=True)


def multiply_last(core, left, total, last, cut, end, name):
    rows, columns = total.shape[0] // 2, end - cut
    shape = jax.ShapeDtypeStruct((rows, columns), left.dtype)
    vmem = pl.BlockSpec(memory_space=pltpu.VMEM)
    return pl.pallas_call(
        functools.partial(last_kernel, cut, 256),
        out_shape=(shape, shape),
        in_specs=[pl.BlockSpec(memory_space=pltpu.SMEM)] + [vmem] * (2 + len(last)),
        out_specs=(vmem, vmem),
        compiler_params=pltpu.CompilerParams(vmem_limit_bytes=14 << 20),
        cost_estimate=pl.CostEstimate(flops=1024 * rows * columns, bytes_accessed=6 << 20, transcendentals=0),
        name=name,
    )(core, left, total, *last)


def put_kernel(got, core_ref, half_0, half_1, *refs):
    gate_ref, up_ref, sems = refs[-3:]

    def put(out):
        copies = []
        for k, (half, at) in enumerate(((half_0, 0), (half_1, half_0.shape[1]))):
            copies.append(pltpu.make_async_copy(half, out.at[:, pl.ds(at, half.shape[1])], sems.at[k]))
        for copy in copies:
            copy.start()
        for copy in copies:
            copy.wait()

    @pl.when(core_ref[0] == got)
    def _():
        put(gate_ref)

    @pl.when(core_ref[0] == 1 - got)
    def _():
        put(up_ref)


def put(core, half_0, half_1, outs, got):
    rows, columns = half_0.shape[0], half_0.shape[1] + half_1.shape[1]
    shape = jax.ShapeDtypeStruct((rows, columns), half_0.dtype)
    anywhere = pl.BlockSpec(memory_space=pl.ANY)
    return pl.pallas_call(
        functools.partial(put_kernel, got),
        out_shape=(shape, shape),
        in_specs=[pl.BlockSpec(memory_space=pltpu.SMEM)] + [anywhere] * (2 + len(outs)),
        out_specs=(anywhere, anywhere),
        scratch_shapes=[pltpu.SemaphoreType.DMA((2,))],
        input_output_aliases={3 + k: k for k in range(len(outs))},
        compiler_params=pltpu.CompilerParams(vmem_limit_bytes=4 << 20),
        cost_estimate=pl.CostEstimate(flops=0, bytes_accessed=4 << 20, transcendentals=0),
        name="put_got" if got else "put_keep",
    )(core, half_0, half_1, *outs)


def weigh(left, coef):
    return (coef[:, None, None] * left.astype(jnp.float32)).astype(jnp.bfloat16)


def shards(gate_left, up_left, gate_right, up_right, fitness_order, member_scale):
    y, z, core = lax.axis_index("y"), lax.axis_index("z"), lax.axis_index("c")
    first = core == 0
    place = jnp.stack([lax.axis_index("x"), y, z, lax.axis_index("h")]).astype(jnp.int32)
    token = core.reshape(1).astype(jnp.int32)
    total = Y * Z * C * H * X
    rank, columns = gate_right.shape[1:]

    def event(*arrived):
        nonlocal token
        *arrived, token = lax.optimization_barrier((*arrived, token))
        return arrived

    gate_got, up_got = shift(gate_right, "c", 1), shift(up_right, "c", 1)
    centered = (2 * fitness_order - (total - 1)).astype(jnp.float32)
    coef = centered * member_scale / ((total - 1) * math.sqrt(total * rank))
    gate_w, up_w = weigh(gate_left, coef)[0], weigh(up_left, coef)[0]
    left_mine, left_send = jnp.where(first, gate_w, up_w), jnp.where(first, up_w, gate_w)
    gate_got, up_got, left_mine, left_send, place = event(gate_got, up_got, left_mine, left_send, place)
    own = jnp.concatenate([jnp.where(first, gate_right, up_got), jnp.where(first, gate_got, up_right)], axis=1)
    own = own.reshape(-1, columns)
    left_got = shift(left_send, "c", 1)
    left = jnp.concatenate([jnp.where(first, left_mine, left_got), jnp.where(first, left_got, left_mine)], axis=0)

    def deal(block, axis, at, size):
        width = block.shape[-1] // size
        parts = []
        for by in range(size):
            start = lax.rem(at + by, size) * width
            part = lax.dynamic_slice_in_dim(block, start, width, axis=block.ndim - 1)
            parts.append(shift(part, axis, by) if by else part)
        return parts

    n = own.shape[0]
    half = n // 2

    def both(block, up=None, down=None):
        if up is not None:
            up, down = join(block, up, down)
        else:
            up = down = block
        return shift(up, "y", 1), shift(down, "y", -1)

    def join(block, up, down):
        return jnp.concatenate([block, up[:half]], axis=0), jnp.concatenate([block, down[half:n]], axis=0)

    left = left.reshape(C * rank, Y * Z, -1).transpose(1, 0, 2)
    left = lax.all_to_all(left, ("y", "z"), split_axis=0, concat_axis=0, tiled=True)
    own, = event(own)
    up0, down0 = both(own)
    z1 = shift(own, "z", 1)
    up0, down0, z1 = event(up0, down0, z1)

    up1, down1 = join(z1, up0, down0)
    up1 = shift(up1, "y", 1)
    z2 = shift(z1, "z", 1)
    left, down1 = event(left, down1)
    down1 = shift(down1, "y", -1)
    left_h = shift(left, "h", 1)
    up1, down1, z2, left, left_h = event(up1, down1, z2, left, left_h)

    up2, down2 = both(z2, up1, down1)
    z3 = shift(z2, "z", 1)
    left = jnp.stack([left, left_h])
    left_1, left_3 = shift(left, "x", 1), shift(left, "x", 3)
    up2, down2, z3, left, left_1, left_3 = event(up2, down2, z3, left, left_1, left_3)

    up3, down3 = both(z3, up2, down2)
    left_0, left_1, left_2 = arrange_left(place, [left, left_1, shift(left, "x", 2), left_3])

    def slot(block, up, down, up_next, down_next):
        return [(block, 0, n), (up, 0, n), (down, 0, n), (up_next, n, half), (down_next, n, half)]

    total = multiply_part(left_0, slot(own, up0, down0, up1, down1) + slot(z1, up1, down1, up2, down2), None, "multiply_0")
    up3, down3, total = event(up3, down3, total)

    up4, down4 = shift(up3[:half], "y", 1), shift(down3[half:n], "y", -1)
    pieces = slot(z2, up2, down2, up3, down3) + [(z3, 0, n), (up3, 0, n), (down3, 0, n)]
    total = multiply_part(left_1, pieces, total, "multiply_1")
    up4, down4, total = event(up4, down4, total)
    cut = columns // 2
    keep_0, send_0 = multiply_last(token, left_2, total, [up4, down4], 0, cut, "multiply_2")
    got_0 = shift(send_0, "c", 1)
    keep_1, send_1 = multiply_last(token, left_2, total, [up4, down4], cut, columns, "multiply_3")
    got_0, send_1 = event(got_0, send_1)
    got_1 = shift(send_1, "c", 1)
    outs = put(token, keep_0, keep_1, [], 0)
    return tuple(put(token, got_0, got_1, outs, 1))


def solution(mesh):
    fine = Mesh(mesh.devices.reshape(Y, Z, C, H, X), ("y", "z", "c", "h", "x"))
    pop, tp = ("y", "z", "c"), ("h", "x")
    in_specs = (
        P(pop + tp, None, None),
        P(pop + tp, None, None),
        P(pop, None, tp),
        P(pop, None, tp),
        P(pop + tp),
        P(pop + tp),
    )
    out_specs = (P(pop, tp), P(pop, tp))
    return jax.shard_map(shards, mesh=fine, in_specs=in_specs, out_specs=out_specs, check_vma=False)
```

```python
import functools
import math

import jax
import jax.numpy as jnp
from jax import lax
from jax.experimental import pallas as pl
from jax.experimental.pallas import tpu as pltpu
from jax.sharding import Mesh, PartitionSpec as P

Y, Z, C, H, X = 4, 4, 2, 2, 4
ORDER = (
    ((0, 0), (0, 1), (0, 3), (0, 2)),
    ((1, 0), (1, 1), (1, 3), (1, 2)),
    ((2, 0), (2, 1), (2, 3), (3, 0)),
    ((2, 2), (3, 1), (3, 3), (3, 2)),
)


def shift(x, axis, by):
    n = lax.axis_size(axis)
    return lax.ppermute(x, axis, [(i, (i + by) % n) for i in range(n)])


def left_kernel(place_ref, *refs):
    *left_refs, out_ref, last_ref, held = refs
    x, y, z, h = place_ref[0], place_ref[1], place_ref[2], place_ref[3]
    for r, left_ref in enumerate(left_refs):
        held[r] = left_ref[...].astype(held.dtype)
    for k, order in enumerate(ORDER):
        parts = []
        for d, from_y in order:
            chip = lax.rem(y + Y - from_y, Y) * Z + lax.rem(z + Z - d, Z)
            for at_h in range(H):
                for at_x in range(X):
                    parts.append(held[lax.rem(x + X - at_x, X), lax.rem(h + at_h, H), chip])
        block = jnp.concatenate(parts, axis=0).T.astype(out_ref.dtype)
        if k < len(ORDER) - 1:
            out_ref[:, k * block.shape[1] : (k + 1) * block.shape[1]] = block
        else:
            last_ref[...] = block


def arrange_left(place, lefts):
    rows = lefts[0].shape[-1]
    size = H * X * lefts[0].shape[2]
    vmem = pl.BlockSpec(memory_space=pltpu.VMEM)
    return pl.pallas_call(
        left_kernel,
        out_shape=(
            jax.ShapeDtypeStruct((rows, (Z - 1) * Y * size), lefts[0].dtype),
            jax.ShapeDtypeStruct((rows, Y * size), lefts[0].dtype),
        ),
        in_specs=[pl.BlockSpec(memory_space=pltpu.SMEM)] + [vmem] * X,
        out_specs=(vmem, vmem),
        scratch_shapes=[pltpu.VMEM((X,) + lefts[0].shape, jnp.float32)],
        compiler_params=pltpu.CompilerParams(vmem_limit_bytes=8 << 20),
        cost_estimate=pl.CostEstimate(flops=0, bytes_accessed=6 << 20, transcendentals=0),
        name="arrange_left",
    )(place, *lefts)


def part_kernel(ranges, width, left_ref, *refs):
    *arrays, out_ref, held, sems = refs
    total_ref = arrays.pop() if len(arrays) > len({which for which, _, _ in ranges}) else None
    columns = out_ref.shape[1]
    cuts = (0, columns // (2 * width) * width, columns)

    def copies(side):
        found, at = [], 0
        part = pl.ds(cuts[side], cuts[side + 1] - cuts[side])
        for which, row, count in ranges:
            source, target = arrays[which].at[pl.ds(row, count), part], held.at[pl.ds(at, count), part]
            found.append(pltpu.make_async_copy(source, target, sems.at[side, len(found)]))
            at += count
        return found

    for side in (0, 1):
        for copy in copies(side):
            copy.start()
    for side in (0, 1):
        for copy in copies(side):
            copy.wait()

        def step(i, _):
            at = pl.ds(pl.multiple_of(i * width, width), width)
            product = jnp.dot(left_ref[...], held[:, at], preferred_element_type=jnp.float32)
            out_ref[:, at] = product if total_ref is None else total_ref[:, at] + product
            return _

        lax.fori_loop(cuts[side] // width, cuts[side + 1] // width, step, None, unroll=True)


def multiply_part(left, pieces, total, name):
    arrays, ranges = [], []
    for array, row, count in pieces:
        known = [k for k, other in enumerate(arrays) if other is array]
        if not known:
            arrays.append(array)
        ranges.append((known[0] if known else len(arrays) - 1, row, count))
    rows, depth = left.shape
    columns = arrays[0].shape[1]
    vmem = pl.BlockSpec(memory_space=pltpu.VMEM)
    totals = [] if total is None else [total]
    return pl.pallas_call(
        functools.partial(part_kernel, ranges, 256),
        out_shape=jax.ShapeDtypeStruct((rows, columns), jnp.float32),
        in_specs=[vmem] + [pl.BlockSpec(memory_space=pl.ANY)] * len(arrays) + [vmem] * len(totals),
        out_specs=vmem,
        scratch_shapes=[
            pltpu.VMEM((depth, columns), left.dtype),
            pltpu.SemaphoreType.DMA((2, len(ranges))),
        ],
        input_output_aliases={1 + len(arrays): 0} if totals else {},
        compiler_params=pltpu.CompilerParams(vmem_limit_bytes=24 << 20),
        cost_estimate=pl.CostEstimate(
            flops=4 * rows * columns * depth, bytes_accessed=12 << 20, transcendentals=0
        ),
        name=name,
    )(left, *arrays, *totals)


def last_kernel(ranges, cut, width, core_ref, left_ref, total_ref, *refs):
    *right_refs, keep_ref, send_ref = refs
    rows, columns = keep_ref.shape
    mine = pl.multiple_of(core_ref[0] * rows, rows)
    other = pl.multiple_of((1 - core_ref[0]) * rows, rows)

    def step(i, _):
        at = pl.ds(pl.multiple_of(i * width, width), width)
        from_at = pl.ds(pl.multiple_of(cut + i * width, width), width)
        right = jnp.concatenate([right_refs[k][pl.ds(row, count), from_at] for k, row, count in ranges], axis=0)
        for out_ref, row in ((send_ref, other), (keep_ref, mine)):
            total = total_ref[pl.ds(row, rows), from_at]
            total += jnp.dot(left_ref[pl.ds(row, rows)], right, preferred_element_type=jnp.float32)
            out_ref[:, at] = total.astype(out_ref.dtype)
        return _

    lax.fori_loop(0, columns // width, step, None, unroll=True)


def multiply_last(core, left, total, arrays, ranges, cut, end, name):
    rows, columns = total.shape[0] // 2, end - cut
    shape = jax.ShapeDtypeStruct((rows, columns), left.dtype)
    vmem = pl.BlockSpec(memory_space=pltpu.VMEM)
    return pl.pallas_call(
        functools.partial(last_kernel, ranges, cut, 256),
        out_shape=(shape, shape),
        in_specs=[pl.BlockSpec(memory_space=pltpu.SMEM)] + [vmem] * (2 + len(arrays)),
        out_specs=(vmem, vmem),
        compiler_params=pltpu.CompilerParams(vmem_limit_bytes=14 << 20),
        cost_estimate=pl.CostEstimate(flops=1024 * rows * columns, bytes_accessed=6 << 20, transcendentals=0),
        name=name,
    )(core, left, total, *arrays)


def put_kernel(got, at, core_ref, part_ref, *refs):
    gate_ref, up_ref, sem = refs[-3:]

    def put(out_ref):
        copy = pltpu.make_async_copy(part_ref, out_ref.at[:, pl.ds(at, part_ref.shape[1])], sem)
        copy.start()
        copy.wait()

    @pl.when(core_ref[0] == got)
    def _():
        put(gate_ref)

    @pl.when(core_ref[0] == 1 - got)
    def _():
        put(up_ref)


def put(core, part, outs, got, at, columns):
    shape = jax.ShapeDtypeStruct((part.shape[0], columns), part.dtype)
    anywhere = pl.BlockSpec(memory_space=pl.ANY)
    return pl.pallas_call(
        functools.partial(put_kernel, got, at),
        out_shape=(shape, shape),
        in_specs=[pl.BlockSpec(memory_space=pltpu.SMEM)] + [anywhere] * (1 + len(outs)),
        out_specs=(anywhere, anywhere),
        scratch_shapes=[pltpu.SemaphoreType.DMA],
        input_output_aliases={2 + k: k for k in range(len(outs))},
        compiler_params=pltpu.CompilerParams(vmem_limit_bytes=4 << 20),
        cost_estimate=pl.CostEstimate(flops=0, bytes_accessed=4 << 20, transcendentals=0),
        name=f"put_{got}_{at}",
    )(core, part, *outs)


def weigh(left, coef):
    return (coef[:, None, None] * left.astype(jnp.float32)).astype(jnp.bfloat16)


def shards(gate_left, up_left, gate_right, up_right, fitness_order, member_scale):
    y, z, core = lax.axis_index("y"), lax.axis_index("z"), lax.axis_index("c")
    first = core == 0
    place = jnp.stack([lax.axis_index("x"), y, z, lax.axis_index("h")]).astype(jnp.int32)
    token = core.reshape(1).astype(jnp.int32)
    total = Y * Z * C * H * X
    rank, columns = gate_right.shape[1:]

    def event(*arrived):
        nonlocal token
        *arrived, token = lax.optimization_barrier((*arrived, token))
        return arrived

    gate_got, up_got = shift(gate_right, "c", 1), shift(up_right, "c", 1)
    centered = (2 * fitness_order - (total - 1)).astype(jnp.float32)
    coef = centered * member_scale / ((total - 1) * math.sqrt(total * rank))
    gate_w, up_w = weigh(gate_left, coef)[0], weigh(up_left, coef)[0]
    left_mine, left_send = jnp.where(first, gate_w, up_w), jnp.where(first, up_w, gate_w)
    gate_got, up_got, left_mine, left_send, place = event(gate_got, up_got, left_mine, left_send, place)
    own = jnp.concatenate([jnp.where(first, gate_right, up_got), jnp.where(first, gate_got, up_right)], axis=1)
    own = own.reshape(-1, columns)
    left_got = shift(left_send, "c", 1)
    left = jnp.concatenate([jnp.where(first, left_mine, left_got), jnp.where(first, left_got, left_mine)], axis=0)

    def deal(block, axis, at, size):
        width = block.shape[-1] // size
        parts = []
        for by in range(size):
            start = lax.rem(at + by, size) * width
            part = lax.dynamic_slice_in_dim(block, start, width, axis=block.ndim - 1)
            parts.append(shift(part, axis, by) if by else part)
        return parts

    n = own.shape[0]
    half = n // 2

    def both(block, up=None, down=None):
        if up is not None:
            up, down = join(block, up, down)
        else:
            up = down = block
        return shift(up, "y", 1), shift(down, "y", -1)

    def join(block, up, down):
        return jnp.concatenate([block, up[:half]], axis=0), jnp.concatenate([block, down[half:n]], axis=0)

    left = left.reshape(C * rank, Y * Z, -1).transpose(1, 0, 2)
    left = lax.all_to_all(left, ("y", "z"), split_axis=0, concat_axis=0, tiled=True)
    own, = event(own)
    up0, down0 = both(own)
    z1 = shift(own, "z", 1)
    up0, down0, z1 = event(up0, down0, z1)

    up1, down1 = join(z1, up0, down0)
    up1 = shift(up1, "y", 1)
    z2 = shift(z1, "z", 1)
    left, down1 = event(left, down1)
    down1 = shift(down1, "y", -1)
    left_h = shift(left, "h", 1)
    up1, down1, z2, left, left_h = event(up1, down1, z2, left, left_h)

    up2, down2 = both(z2, up1, down1)
    z3 = shift(z2, "z", 1)
    left = jnp.stack([left, left_h])
    left_1, left_3 = shift(left, "x", 1), shift(left, "x", 3)
    up2, down2, z3, left, left_1, left_3 = event(up2, down2, z3, left, left_1, left_3)

    up3, down3 = both(z3, up2, down2)
    far3 = shift(jnp.concatenate([up1[n:], down1[n:]], axis=0), "z", 3)
    left, left_last = arrange_left(place, [left, left_1, shift(left, "x", 2), left_3])

    def slot(block, up, down, up_next, down_next):
        return [(block, 0, n), (up, 0, n), (down, 0, n), (up_next, n, half), (down_next, n, half)]

    pieces = slot(own, up0, down0, up1, down1) + slot(z1, up1, down1, up2, down2)
    pieces += [(part, 0, n) for part in (z2, up2, down2, z3)]
    total = multiply_part(left, pieces, None, "multiply_0")
    up3, down3, far3, total = event(up3, down3, far3, total)

    cut = columns // 2
    lasts = [up3, down3, far3]
    ranges = [(0, n, half), (1, n, half), (0, 0, n), (1, 0, n), (2, 0, n)]
    keep_0, send_0 = multiply_last(token, left_last, total, lasts, ranges, 0, cut, "multiply_1")
    got_0 = shift(send_0, "c", 1)
    keep_1, send_1 = multiply_last(token, left_last, total, lasts, ranges, cut, columns, "multiply_2")
    outs = put(token, keep_0, [], 0, 0, columns)
    got_0, send_1, *outs = event(got_0, send_1, *outs)
    got_1 = shift(send_1, "c", 1)
    outs = put(token, keep_1, outs, 0, cut, columns)
    outs = put(token, got_0, outs, 1, 0, columns)
    got_1, *outs = event(got_1, *outs)
    return tuple(put(token, got_1, outs, 1, cut, columns))


def solution(mesh):
    fine = Mesh(mesh.devices.reshape(Y, Z, C, H, X), ("y", "z", "c", "h", "x"))
    pop, tp = ("y", "z", "c"), ("h", "x")
    in_specs = (
        P(pop + tp, None, None),
        P(pop + tp, None, None),
        P(pop, None, tp),
        P(pop, None, tp),
        P(pop + tp),
        P(pop + tp),
    )
    out_specs = (P(pop, tp), P(pop, tp))
    return jax.shard_map(shards, mesh=fine, in_specs=in_specs, out_specs=out_specs, check_vma=False)
```

```python
import functools
import math

import jax
import jax.numpy as jnp
from jax import lax
from jax.experimental import pallas as pl
from jax.experimental.pallas import tpu as pltpu
from jax.sharding import Mesh, PartitionSpec as P

Y, Z, C, H, X = 4, 4, 2, 2, 4
ORDER = (
    ((0, 0), (0, 1), (0, 3), (0, 2)),
    ((1, 0), (1, 1), (1, 3), (1, 2)),
    ((2, 0), (2, 1), (2, 3), (3, 0)),
    ((2, 2), (3, 1), (3, 3), (3, 2)),
)


def shift(x, axis, by):
    n = lax.axis_size(axis)
    return lax.ppermute(x, axis, [(i, (i + by) % n) for i in range(n)])


def left_kernel(place_ref, *refs):
    *left_refs, out_ref, last_ref, held = refs
    x, y, z, h = place_ref[0], place_ref[1], place_ref[2], place_ref[3]
    for r, left_ref in enumerate(left_refs):
        held[r] = left_ref[...].astype(held.dtype)
    for k, order in enumerate(ORDER):
        parts = []
        for d, from_y in order:
            chip = lax.rem(y + Y - from_y, Y) * Z + lax.rem(z + Z - d, Z)
            for at_h in range(H):
                for at_x in range(X):
                    parts.append(held[lax.rem(x + X - at_x, X), lax.rem(h + at_h, H), chip])
        block = jnp.concatenate(parts, axis=0).T.astype(out_ref.dtype)
        if k < len(ORDER) - 1:
            out_ref[:, k * block.shape[1] : (k + 1) * block.shape[1]] = block
        else:
            last_ref[...] = block


def arrange_left(place, lefts):
    rows = lefts[0].shape[-1]
    size = H * X * lefts[0].shape[2]
    vmem = pl.BlockSpec(memory_space=pltpu.VMEM)
    return pl.pallas_call(
        left_kernel,
        out_shape=(
            jax.ShapeDtypeStruct((rows, (Z - 1) * Y * size), lefts[0].dtype),
            jax.ShapeDtypeStruct((rows, Y * size), lefts[0].dtype),
        ),
        in_specs=[pl.BlockSpec(memory_space=pltpu.SMEM)] + [vmem] * X,
        out_specs=(vmem, vmem),
        scratch_shapes=[pltpu.VMEM((X,) + lefts[0].shape, jnp.float32)],
        compiler_params=pltpu.CompilerParams(vmem_limit_bytes=8 << 20),
        cost_estimate=pl.CostEstimate(flops=0, bytes_accessed=6 << 20, transcendentals=0),
        name="arrange_left",
    )(place, *lefts)


def part_kernel(ranges, width, left_ref, *refs):
    *arrays, out_ref = refs
    left = left_ref[...]
    for at in range(0, out_ref.shape[1], width):
        columns = slice(at, at + width)
        right = jnp.concatenate([arrays[which][row : row + count, columns] for which, row, count in ranges], axis=0)
        out_ref[:, columns] = jnp.dot(left, right, preferred_element_type=jnp.float32)


def multiply_part(left, pieces, name):
    arrays, ranges = [], []
    for array, row, count in pieces:
        known = [k for k, other in enumerate(arrays) if other is array]
        if not known:
            arrays.append(array)
        ranges.append((known[0] if known else len(arrays) - 1, row, count))
    rows, depth = left.shape
    columns = arrays[0].shape[1]
    vmem = pl.BlockSpec(memory_space=pltpu.VMEM)
    return pl.pallas_call(
        functools.partial(part_kernel, ranges, 256),
        out_shape=jax.ShapeDtypeStruct((rows, columns), jnp.float32),
        in_specs=[vmem] * (1 + len(arrays)),
        out_specs=vmem,
        compiler_params=pltpu.CompilerParams(vmem_limit_bytes=24 << 20),
        cost_estimate=pl.CostEstimate(
            flops=2 * rows * columns * depth, bytes_accessed=1 << 20, transcendentals=0
        ),
        name=name,
    )(left, *arrays)


def last_kernel(mine, ranges, width, core_ref, left_ref, total_ref, *refs):
    right_refs, out_refs = refs[:3], refs[3:]
    rows = out_refs[0].shape[0]
    core = core_ref[0] if mine else 1 - core_ref[0]
    row = pl.ds(pl.multiple_of(core * rows, rows), rows)
    start = 0
    for out_ref in out_refs:
        for at in range(0, out_ref.shape[1], width):
            from_at = slice(start + at, start + at + width)
            right = jnp.concatenate([right_refs[k][first : first + count, from_at] for k, first, count in ranges], axis=0)
            total = total_ref[row, from_at]
            total += jnp.dot(left_ref[row], right, preferred_element_type=jnp.float32)
            out_ref[:, at : at + width] = total.astype(out_ref.dtype)
        start += out_ref.shape[1]


def multiply_last(core, left, total, arrays, ranges, mine, cuts, name):
    rows = total.shape[0] // 2
    vmem = pl.BlockSpec(memory_space=pltpu.VMEM)
    return pl.pallas_call(
        functools.partial(last_kernel, mine, ranges, 256),
        out_shape=tuple(jax.ShapeDtypeStruct((rows, cut), left.dtype) for cut in cuts),
        in_specs=[pl.BlockSpec(memory_space=pltpu.SMEM)] + [vmem] * (2 + len(arrays)),
        out_specs=(vmem,) * len(cuts),
        compiler_params=pltpu.CompilerParams(vmem_limit_bytes=14 << 20),
        cost_estimate=pl.CostEstimate(flops=1024 * rows * sum(cuts), bytes_accessed=6 << 20, transcendentals=0),
        name=name,
    )(core, left, total, *arrays)


def put_kernel(got, at, core_ref, part_ref, *refs):
    gate_ref, up_ref, sem = refs[-3:]

    def put(out_ref):
        copy = pltpu.make_async_copy(part_ref, out_ref.at[:, pl.ds(at, part_ref.shape[1])], sem)
        copy.start()
        copy.wait()

    @pl.when(core_ref[0] == got)
    def _():
        put(gate_ref)

    @pl.when(core_ref[0] == 1 - got)
    def _():
        put(up_ref)


def put(core, part, outs, got, at, columns):
    shape = jax.ShapeDtypeStruct((part.shape[0], columns), part.dtype)
    anywhere = pl.BlockSpec(memory_space=pl.ANY)
    return pl.pallas_call(
        functools.partial(put_kernel, got, at),
        out_shape=(shape, shape),
        in_specs=[pl.BlockSpec(memory_space=pltpu.SMEM)] + [anywhere] * (1 + len(outs)),
        out_specs=(anywhere, anywhere),
        scratch_shapes=[pltpu.SemaphoreType.DMA],
        input_output_aliases={2 + k: k for k in range(len(outs))},
        compiler_params=pltpu.CompilerParams(vmem_limit_bytes=4 << 20),
        cost_estimate=pl.CostEstimate(flops=0, bytes_accessed=4 << 20, transcendentals=0),
        name=f"put_{got}_{at}",
    )(core, part, *outs)


def weigh(left, coef):
    return (coef[:, None, None] * left.astype(jnp.float32)).astype(jnp.bfloat16)


def shards(gate_left, up_left, gate_right, up_right, fitness_order, member_scale):
    y, z, core = lax.axis_index("y"), lax.axis_index("z"), lax.axis_index("c")
    first = core == 0
    place = jnp.stack([lax.axis_index("x"), y, z, lax.axis_index("h")]).astype(jnp.int32)
    token = core.reshape(1).astype(jnp.int32)
    total = Y * Z * C * H * X
    rank, columns = gate_right.shape[1:]

    def event(*arrived):
        nonlocal token
        *arrived, token = lax.optimization_barrier((*arrived, token))
        return arrived

    gate_got, up_got = shift(gate_right, "c", 1), shift(up_right, "c", 1)
    centered = (2 * fitness_order - (total - 1)).astype(jnp.float32)
    coef = centered * member_scale / ((total - 1) * math.sqrt(total * rank))
    gate_w, up_w = weigh(gate_left, coef)[0], weigh(up_left, coef)[0]
    left_mine, left_send = jnp.where(first, gate_w, up_w), jnp.where(first, up_w, gate_w)
    gate_got, up_got, left_mine, left_send, place = event(gate_got, up_got, left_mine, left_send, place)
    own = jnp.concatenate([jnp.where(first, gate_right, up_got), jnp.where(first, gate_got, up_right)], axis=1)
    own = own.reshape(-1, columns)
    left_got = shift(left_send, "c", 1)
    left = jnp.concatenate([jnp.where(first, left_mine, left_got), jnp.where(first, left_got, left_mine)], axis=0)

    def deal(block, axis, at, size):
        width = block.shape[-1] // size
        parts = []
        for by in range(size):
            start = lax.rem(at + by, size) * width
            part = lax.dynamic_slice_in_dim(block, start, width, axis=block.ndim - 1)
            parts.append(shift(part, axis, by) if by else part)
        return parts

    n = own.shape[0]
    half = n // 2

    def both(block, up=None, down=None):
        if up is not None:
            up, down = join(block, up, down)
        else:
            up = down = block
        return shift(up, "y", 1), shift(down, "y", -1)

    def join(block, up, down):
        return jnp.concatenate([block, up[:half]], axis=0), jnp.concatenate([block, down[half:n]], axis=0)

    left = left.reshape(C * rank, Y * Z, -1).transpose(1, 0, 2)
    left = lax.all_to_all(left, ("y", "z"), split_axis=0, concat_axis=0, tiled=True)
    own, = event(own)
    up0, down0 = both(own)
    z1 = shift(own, "z", 1)
    z1, down0, up0 = event(z1, down0, up0)

    up1, down1 = join(z1, up0, down0)
    up1 = shift(up1, "y", 1)
    z2 = shift(z1, "z", 1)
    left, down1 = event(left, down1)
    down1 = shift(down1, "y", -1)
    left_h = shift(left, "h", 1)
    z2, left, left_h, down1, up1 = event(z2, left, left_h, down1, up1)

    up2, down2 = both(z2, up1, down1)
    z3 = shift(z2, "z", 1)
    left = jnp.stack([left, left_h])
    left_1, left_3 = shift(left, "x", 1), shift(left, "x", 3)
    z3, left, left_1, left_3, down2, up2 = event(z3, left, left_1, left_3, down2, up2)

    up3, down3 = both(z3, up2, down2)
    far3 = shift(jnp.concatenate([up1[n:], down1[n:]], axis=0), "z", 3)
    left, left_last = arrange_left(place, [left, left_1, shift(left, "x", 2), left_3])

    def slot(block, up, down, up_next, down_next):
        return [(block, 0, n), (up, 0, n), (down, 0, n), (up_next, n, half), (down_next, n, half)]

    pieces = slot(own, up0, down0, up1, down1) + slot(z1, up1, down1, up2, down2)
    pieces += [(part, 0, n) for part in (z2, up2, down2, z3)]
    total = multiply_part(left, pieces, "multiply_0")
    far3, down3, up3, total = event(far3, down3, up3, total)

    cut = columns // 2
    lasts = [up3, down3, far3]
    ranges = [(0, n, half), (1, n, half), (0, 0, n), (1, 0, n), (2, 0, n)]
    cuts = (cut, columns - cut)
    sends = multiply_last(token, left_last, total, lasts, ranges, False, cuts, "multiply_1")
    got_0, got_1 = [shift(send, "c", 1) for send in sends]
    (keep,) = multiply_last(token, left_last, total, lasts, ranges, True, (columns,), "multiply_2")
    outs = put(token, keep, [], 0, 0, columns)
    got_0, *outs = event(got_0, *outs)
    outs = put(token, got_0, outs, 1, 0, columns)
    got_1, *outs = event(got_1, *outs)
    return tuple(put(token, got_1, outs, 1, cut, columns))


def solution(mesh):
    fine = Mesh(mesh.devices.reshape(Y, Z, C, H, X), ("y", "z", "c", "h", "x"))
    pop, tp = ("y", "z", "c"), ("h", "x")
    in_specs = (
        P(pop + tp, None, None),
        P(pop + tp, None, None),
        P(pop, None, tp),
        P(pop, None, tp),
        P(pop + tp),
        P(pop + tp),
    )
    out_specs = (P(pop, tp), P(pop, tp))
    return jax.shard_map(shards, mesh=fine, in_specs=in_specs, out_specs=out_specs, check_vma=False)
```

```python
import functools
import math

import jax
import jax.numpy as jnp
from jax import lax
from jax.experimental import pallas as pl
from jax.experimental.pallas import tpu as pltpu
from jax.sharding import Mesh, PartitionSpec as P

Y, Z, C, H, X = 4, 4, 2, 2, 4
ORDER = (
    ((0, 0), (0, 1), (0, 3), (0, 2)),
    ((1, 0), (1, 1), (1, 3), (1, 2)),
    ((2, 0), (2, 1), (2, 3), (3, 0)),
    ((2, 2), (3, 1), (3, 3), (3, 2)),
)


def shift(x, axis, by):
    n = lax.axis_size(axis)
    return lax.ppermute(x, axis, [(i, (i + by) % n) for i in range(n)])


def left_kernel(place_ref, *refs):
    *left_refs, out_ref, last_ref, held = refs
    x, y, z = place_ref[0], place_ref[1], place_ref[2]
    for r, left_ref in enumerate(left_refs):
        held[r] = left_ref[...].astype(held.dtype)
    for k, order in enumerate(ORDER):
        parts = []
        for d, from_y in order:
            chip = lax.rem(y + Y - from_y, Y) * Z + lax.rem(z + Z - d, Z)
            for at_h in range(H):
                for at_x in range(X):
                    parts.append(held[lax.rem(x + X - at_x, X), at_h * Y * Z + chip])
        block = jnp.concatenate(parts, axis=0).T.astype(out_ref.dtype)
        if k < len(ORDER) - 1:
            out_ref[:, k * block.shape[1] : (k + 1) * block.shape[1]] = block
        else:
            last_ref[...] = block


def arrange_left(place, lefts):
    rows = lefts[0].shape[-1]
    size = H * X * lefts[0].shape[1]
    vmem = pl.BlockSpec(memory_space=pltpu.VMEM)
    return pl.pallas_call(
        left_kernel,
        out_shape=(
            jax.ShapeDtypeStruct((rows, (Z - 1) * Y * size), lefts[0].dtype),
            jax.ShapeDtypeStruct((rows, Y * size), lefts[0].dtype),
        ),
        in_specs=[pl.BlockSpec(memory_space=pltpu.SMEM)] + [vmem] * X,
        out_specs=(vmem, vmem),
        scratch_shapes=[pltpu.VMEM((X,) + lefts[0].shape, jnp.float32)],
        compiler_params=pltpu.CompilerParams(vmem_limit_bytes=8 << 20),
        cost_estimate=pl.CostEstimate(flops=0, bytes_accessed=6 << 20, transcendentals=0),
        name="arrange_left",
    )(place, *lefts)


def part_kernel(ranges, width, left_ref, *refs):
    *arrays, out_ref = refs
    left = left_ref[...]
    for at in range(0, out_ref.shape[1], width):
        columns = slice(at, at + width)
        right = jnp.concatenate([arrays[which][row : row + count, columns] for which, row, count in ranges], axis=0)
        out_ref[:, columns] = jnp.dot(left, right, preferred_element_type=jnp.float32)


def multiply_part(left, pieces, name):
    arrays, ranges = [], []
    for array, row, count in pieces:
        known = [k for k, other in enumerate(arrays) if other is array]
        if not known:
            arrays.append(array)
        ranges.append((known[0] if known else len(arrays) - 1, row, count))
    rows, depth = left.shape
    columns = arrays[0].shape[1]
    vmem = pl.BlockSpec(memory_space=pltpu.VMEM)
    return pl.pallas_call(
        functools.partial(part_kernel, ranges, 256),
        out_shape=jax.ShapeDtypeStruct((rows, columns), jnp.float32),
        in_specs=[vmem] * (1 + len(arrays)),
        out_specs=vmem,
        compiler_params=pltpu.CompilerParams(vmem_limit_bytes=24 << 20),
        cost_estimate=pl.CostEstimate(
            flops=2 * rows * columns * depth, bytes_accessed=1 << 20, transcendentals=0
        ),
        name=name,
    )(left, *arrays)


def last_kernel(mine, ranges, width, core_ref, left_ref, total_ref, *refs):
    right_refs, out_refs = refs[:3], refs[3:]
    rows = out_refs[0].shape[0]
    core = core_ref[0] if mine else 1 - core_ref[0]
    row = pl.ds(pl.multiple_of(core * rows, rows), rows)
    start = 0
    for out_ref in out_refs:
        for at in range(0, out_ref.shape[1], width):
            from_at = slice(start + at, start + at + width)
            right = jnp.concatenate([right_refs[k][first : first + count, from_at] for k, first, count in ranges], axis=0)
            total = total_ref[row, from_at]
            total += jnp.dot(left_ref[row], right, preferred_element_type=jnp.float32)
            out_ref[:, at : at + width] = total.astype(out_ref.dtype)
        start += out_ref.shape[1]


def multiply_last(core, left, total, arrays, ranges, mine, cuts, name):
    rows = total.shape[0] // 2
    vmem = pl.BlockSpec(memory_space=pltpu.VMEM)
    return pl.pallas_call(
        functools.partial(last_kernel, mine, ranges, 256),
        out_shape=tuple(jax.ShapeDtypeStruct((rows, cut), left.dtype) for cut in cuts),
        in_specs=[pl.BlockSpec(memory_space=pltpu.SMEM)] + [vmem] * (2 + len(arrays)),
        out_specs=(vmem,) * len(cuts),
        compiler_params=pltpu.CompilerParams(vmem_limit_bytes=14 << 20),
        cost_estimate=pl.CostEstimate(flops=1024 * rows * sum(cuts), bytes_accessed=6 << 20, transcendentals=0),
        name=name,
    )(core, left, total, *arrays)


def put_kernel(got, at, core_ref, part_ref, *refs):
    gate_ref, up_ref, sem = refs[-3:]

    def put(out_ref):
        copy = pltpu.make_async_copy(part_ref, out_ref.at[:, pl.ds(at, part_ref.shape[1])], sem)
        copy.start()
        copy.wait()

    @pl.when(core_ref[0] == got)
    def _():
        put(gate_ref)

    @pl.when(core_ref[0] == 1 - got)
    def _():
        put(up_ref)


def put(core, part, outs, got, at, columns):
    shape = jax.ShapeDtypeStruct((part.shape[0], columns), part.dtype)
    anywhere = pl.BlockSpec(memory_space=pl.ANY)
    return pl.pallas_call(
        functools.partial(put_kernel, got, at),
        out_shape=(shape, shape),
        in_specs=[pl.BlockSpec(memory_space=pltpu.SMEM)] + [anywhere] * (1 + len(outs)),
        out_specs=(anywhere, anywhere),
        scratch_shapes=[pltpu.SemaphoreType.DMA],
        input_output_aliases={2 + k: k for k in range(len(outs))},
        compiler_params=pltpu.CompilerParams(vmem_limit_bytes=4 << 20),
        cost_estimate=pl.CostEstimate(flops=0, bytes_accessed=4 << 20, transcendentals=0),
        name=f"put_{got}_{at}",
    )(core, part, *outs)


def weigh(left, coef):
    return (coef[:, None, None] * left.astype(jnp.float32)).astype(jnp.bfloat16)


def shards(gate_left, up_left, gate_right, up_right, fitness_order, member_scale):
    y, z, core = lax.axis_index("y"), lax.axis_index("z"), lax.axis_index("c")
    first = core == 0
    place = jnp.stack([lax.axis_index("x"), y, z]).astype(jnp.int32)
    token = core.reshape(1).astype(jnp.int32)
    total = Y * Z * C * H * X
    rank, columns = gate_right.shape[1:]

    def event(*arrived):
        nonlocal token
        *arrived, token = lax.optimization_barrier((*arrived, token))
        return arrived

    gate_got, up_got = shift(gate_right, "c", 1), shift(up_right, "c", 1)
    centered = (2 * fitness_order - (total - 1)).astype(jnp.float32)
    coef = centered * member_scale / ((total - 1) * math.sqrt(total * rank))
    gate_w, up_w = weigh(gate_left, coef)[0], weigh(up_left, coef)[0]
    left_mine, left_send = jnp.where(first, gate_w, up_w), jnp.where(first, up_w, gate_w)
    gate_got, up_got, left_mine, left_send, place = event(gate_got, up_got, left_mine, left_send, place)
    own = jnp.concatenate([jnp.where(first, gate_right, up_got), jnp.where(first, gate_got, up_right)], axis=1)
    own = own.reshape(-1, columns)
    left_got = shift(left_send, "c", 1)
    left = jnp.concatenate([jnp.where(first, left_mine, left_got), jnp.where(first, left_got, left_mine)], axis=0)

    def deal(block, axis, at, size):
        width = block.shape[-1] // size
        parts = []
        for by in range(size):
            start = lax.rem(at + by, size) * width
            part = lax.dynamic_slice_in_dim(block, start, width, axis=block.ndim - 1)
            parts.append(shift(part, axis, by) if by else part)
        return parts

    n = own.shape[0]
    half = n // 2

    def both(block, *passing):
        up = jnp.concatenate([block] + [pair[0][:half] for pair in passing], axis=0) if passing else block
        down = jnp.concatenate([block] + [pair[1][half:n] for pair in passing], axis=0) if passing else block
        return shift(up, "y", 1), shift(down, "y", -1)

    left = left.reshape(C * rank, Y * Z, -1).transpose(1, 0, 2)
    left = jnp.concatenate([left, left], axis=0)
    left = lax.all_to_all(left, ("h", "y", "z"), split_axis=0, concat_axis=0, tiled=True)
    own, = event(own)
    up0, down0 = both(own)
    z1 = shift(own, "z", 1)
    z1, down0, up0 = event(z1, down0, up0)

    up1, down1 = both(z1)
    z2 = shift(z1, "z", 1)
    left, = event(left)
    left_1 = shift(left, "x", 1)
    z2, left, left_1, down1, up1 = event(z2, left, left_1, down1, up1)

    up2, down2 = both(z2, (up1, down1), (up0, down0))
    z3 = shift(z2, "z", 1)
    left_2, left_3 = shift(left, "x", 2), shift(left, "x", 3)
    z3, left_2, left_3, down2, up2 = event(z3, left_2, left_3, down2, up2)

    up3, down3 = both(z3, (up2, down2))
    far3 = shift(jnp.concatenate([up2[n + half :], down2[n + half :]], axis=0), "z", 3)
    left, left_last = arrange_left(place, [left, left_1, left_2, left_3])

    def slot(block, up, down, row):
        return [(block, 0, n), (up, 0, n), (down, 0, n), (up2, row, half), (down2, row, half)]

    pieces = slot(own, up0, down0, n + half) + slot(z1, up1, down1, n)
    pieces += [(part, 0, n) for part in (z2, up2, down2, z3)]
    total = multiply_part(left, pieces, "multiply_0")
    far3, down3, up3, total = event(far3, down3, up3, total)

    cut = columns // 2
    lasts = [up3, down3, far3]
    ranges = [(0, n, half), (1, n, half), (0, 0, n), (1, 0, n), (2, 0, n)]
    cuts = (cut, columns - cut)
    sends = multiply_last(token, left_last, total, lasts, ranges, False, cuts, "multiply_1")
    got_0, got_1 = [shift(send, "c", 1) for send in sends]
    (keep,) = multiply_last(token, left_last, total, lasts, ranges, True, (columns,), "multiply_2")
    outs = put(token, keep, [], 0, 0, columns)
    got_0, *outs = event(got_0, *outs)
    outs = put(token, got_0, outs, 1, 0, columns)
    got_1, *outs = event(got_1, *outs)
    return tuple(put(token, got_1, outs, 1, cut, columns))


def solution(mesh):
    fine = Mesh(mesh.devices.reshape(Y, Z, C, H, X), ("y", "z", "c", "h", "x"))
    pop, tp = ("y", "z", "c"), ("h", "x")
    in_specs = (
        P(pop + tp, None, None),
        P(pop + tp, None, None),
        P(pop, None, tp),
        P(pop, None, tp),
        P(pop + tp),
        P(pop + tp),
    )
    out_specs = (P(pop, tp), P(pop, tp))
    return jax.shard_map(shards, mesh=fine, in_specs=in_specs, out_specs=out_specs, check_vma=False)
```

```python
import functools
import math

import jax
import jax.numpy as jnp
from jax import lax
from jax.experimental import pallas as pl
from jax.experimental.pallas import tpu as pltpu
from jax.sharding import Mesh, PartitionSpec as P

Y, Z, C, H, X = 4, 4, 2, 2, 4
ORDER = (
    ((0, 0), (0, 1), (0, 3), (0, 2)),
    ((1, 0), (1, 1), (1, 3), (1, 2)),
    ((2, 0), (2, 1), (2, 3), (3, 0)),
    ((2, 2), (3, 1), (3, 3), (3, 2)),
)


def shift(x, axis, by):
    n = lax.axis_size(axis)
    return lax.ppermute(x, axis, [(i, (i + by) % n) for i in range(n)])


def left_kernel(place_ref, *refs):
    *left_refs, out_ref, last_ref, held = refs
    x, y, z = place_ref[0], place_ref[1], place_ref[2]
    for r, left_ref in enumerate(left_refs):
        held[r] = left_ref[...].astype(held.dtype)
    for k, order in enumerate(ORDER):
        parts = []
        for d, from_y in order:
            chip = lax.rem(y + Y - from_y, Y) * Z + lax.rem(z + Z - d, Z)
            for at_h in range(H):
                for at_x in range(X):
                    parts.append(held[lax.rem(x + X - at_x, X), at_h * Y * Z + chip])
        block = jnp.concatenate(parts, axis=0).T.astype(out_ref.dtype)
        if k < len(ORDER) - 1:
            out_ref[:, k * block.shape[1] : (k + 1) * block.shape[1]] = block
        else:
            last_ref[...] = block


def arrange_left(place, lefts):
    rows = lefts[0].shape[-1]
    size = H * X * lefts[0].shape[1]
    vmem = pl.BlockSpec(memory_space=pltpu.VMEM)
    return pl.pallas_call(
        left_kernel,
        out_shape=(
            jax.ShapeDtypeStruct((rows, (Z - 1) * Y * size), lefts[0].dtype),
            jax.ShapeDtypeStruct((rows, Y * size), lefts[0].dtype),
        ),
        in_specs=[pl.BlockSpec(memory_space=pltpu.SMEM)] + [vmem] * X,
        out_specs=(vmem, vmem),
        scratch_shapes=[pltpu.VMEM((X,) + lefts[0].shape, jnp.float32)],
        compiler_params=pltpu.CompilerParams(vmem_limit_bytes=8 << 20),
        cost_estimate=pl.CostEstimate(flops=0, bytes_accessed=6 << 20, transcendentals=0),
        name="arrange_left",
    )(place, *lefts)


def part_kernel(ranges, width, left_ref, *refs):
    *arrays, out_ref = refs
    left = left_ref[...]
    for at in range(0, out_ref.shape[1], width):
        columns = slice(at, at + width)
        right = jnp.concatenate([arrays[which][row : row + count, columns] for which, row, count in ranges], axis=0)
        out_ref[:, columns] = jnp.dot(left, right, preferred_element_type=jnp.float32)


def multiply_part(left, pieces, name):
    arrays, ranges = [], []
    for array, row, count in pieces:
        known = [k for k, other in enumerate(arrays) if other is array]
        if not known:
            arrays.append(array)
        ranges.append((known[0] if known else len(arrays) - 1, row, count))
    rows, depth = left.shape
    columns = arrays[0].shape[1]
    vmem = pl.BlockSpec(memory_space=pltpu.VMEM)
    return pl.pallas_call(
        functools.partial(part_kernel, ranges, 256),
        out_shape=jax.ShapeDtypeStruct((rows, columns), jnp.float32),
        in_specs=[vmem] * (1 + len(arrays)),
        out_specs=vmem,
        compiler_params=pltpu.CompilerParams(vmem_limit_bytes=24 << 20),
        cost_estimate=pl.CostEstimate(
            flops=2 * rows * columns * depth, bytes_accessed=1 << 20, transcendentals=0
        ),
        name=name,
    )(left, *arrays)


def last_kernel(mine, ranges, width, core_ref, left_ref, total_ref, *refs):
    right_refs, out_refs = refs[:3], refs[3:]
    rows = out_refs[0].shape[0]
    core = core_ref[0] if mine else 1 - core_ref[0]
    row = pl.ds(pl.multiple_of(core * rows, rows), rows)
    start = 0
    for out_ref in out_refs:
        for at in range(0, out_ref.shape[1], width):
            from_at = slice(start + at, start + at + width)
            right = jnp.concatenate([right_refs[k][first : first + count, from_at] for k, first, count in ranges], axis=0)
            total = total_ref[row, from_at]
            total += jnp.dot(left_ref[row], right, preferred_element_type=jnp.float32)
            out_ref[:, at : at + width] = total.astype(out_ref.dtype)
        start += out_ref.shape[1]


def multiply_last(core, left, total, arrays, ranges, mine, cuts, name):
    rows = total.shape[0] // 2
    vmem = pl.BlockSpec(memory_space=pltpu.VMEM)
    return pl.pallas_call(
        functools.partial(last_kernel, mine, ranges, 256),
        out_shape=tuple(jax.ShapeDtypeStruct((rows, cut), left.dtype) for cut in cuts),
        in_specs=[pl.BlockSpec(memory_space=pltpu.SMEM)] + [vmem] * (2 + len(arrays)),
        out_specs=(vmem,) * len(cuts),
        compiler_params=pltpu.CompilerParams(vmem_limit_bytes=14 << 20),
        cost_estimate=pl.CostEstimate(flops=1024 * rows * sum(cuts), bytes_accessed=6 << 20, transcendentals=0),
        name=name,
    )(core, left, total, *arrays)


def put_kernel(got, at, core_ref, part_ref, *refs):
    gate_ref, up_ref, sem = refs[-3:]

    def put(out_ref):
        copy = pltpu.make_async_copy(part_ref, out_ref.at[:, pl.ds(at, part_ref.shape[1])], sem)
        copy.start()
        copy.wait()

    @pl.when(core_ref[0] == got)
    def _():
        put(gate_ref)

    @pl.when(core_ref[0] == 1 - got)
    def _():
        put(up_ref)


def put(core, part, outs, got, at, columns):
    shape = jax.ShapeDtypeStruct((part.shape[0], columns), part.dtype)
    anywhere = pl.BlockSpec(memory_space=pl.ANY)
    return pl.pallas_call(
        functools.partial(put_kernel, got, at),
        out_shape=(shape, shape),
        in_specs=[pl.BlockSpec(memory_space=pltpu.SMEM)] + [anywhere] * (1 + len(outs)),
        out_specs=(anywhere, anywhere),
        scratch_shapes=[pltpu.SemaphoreType.DMA],
        input_output_aliases={2 + k: k for k in range(len(outs))},
        compiler_params=pltpu.CompilerParams(vmem_limit_bytes=4 << 20),
        cost_estimate=pl.CostEstimate(flops=0, bytes_accessed=4 << 20, transcendentals=0),
        name=f"put_{got}_{at}",
    )(core, part, *outs)


def weigh(left, coef):
    return (coef[:, None, None] * left.astype(jnp.float32)).astype(jnp.bfloat16)


def shards(gate_left, up_left, gate_right, up_right, fitness_order, member_scale):
    y, z, core = lax.axis_index("y"), lax.axis_index("z"), lax.axis_index("c")
    first = core == 0
    place = jnp.stack([lax.axis_index("x"), y, z]).astype(jnp.int32)
    token = core.reshape(1).astype(jnp.int32)
    total = Y * Z * C * H * X
    rank, columns = gate_right.shape[1:]

    def event(*arrived):
        nonlocal token
        *arrived, token = lax.optimization_barrier((*arrived, token))
        return arrived

    gate_got, up_got = shift(gate_right, "c", 1), shift(up_right, "c", 1)
    centered = (2 * fitness_order - (total - 1)).astype(jnp.float32)
    coef = centered * member_scale / ((total - 1) * math.sqrt(total * rank))
    gate_w, up_w = weigh(gate_left, coef)[0], weigh(up_left, coef)[0]
    left_mine, left_send = jnp.where(first, gate_w, up_w), jnp.where(first, up_w, gate_w)
    gate_got, up_got, left_mine, left_send, place = event(gate_got, up_got, left_mine, left_send, place)
    own = jnp.concatenate([jnp.where(first, gate_right, up_got), jnp.where(first, gate_got, up_right)], axis=1)
    own = own.reshape(-1, columns)
    left_got = shift(left_send, "c", 1)
    left = jnp.concatenate([jnp.where(first, left_mine, left_got), jnp.where(first, left_got, left_mine)], axis=0)

    def deal(block, axis, at, size):
        width = block.shape[-1] // size
        parts = []
        for by in range(size):
            start = lax.rem(at + by, size) * width
            part = lax.dynamic_slice_in_dim(block, start, width, axis=block.ndim - 1)
            parts.append(shift(part, axis, by) if by else part)
        return parts

    n = own.shape[0]
    half = n // 2

    def both(block):
        return shift(block, "y", 1), shift(block, "y", -1)

    left = left.reshape(C * rank, Y * Z, -1).transpose(1, 0, 2)
    left = jnp.concatenate([left, left], axis=0)
    left = lax.all_to_all(left, ("h", "y", "z"), split_axis=0, concat_axis=0, tiled=True)
    own, = event(own)
    up0, down0 = both(own)
    z1 = shift(own, "z", 1)
    z1, down0, up0 = event(z1, down0, up0)

    up1, down1 = both(z1)
    z2 = shift(z1, "z", 1)
    left, = event(left)
    left_1 = shift(left, "x", 1)
    z2, left, left_1, down1, up1 = event(z2, left, left_1, down1, up1)

    few = n // 4
    up2 = shift(jnp.concatenate([z2[: n - few], up1[:half], up0[:half]], axis=0), "y", 1)
    down2 = shift(jnp.concatenate([z2[few:], down1[half:], down0[half:]], axis=0), "y", -1)
    z3 = shift(jnp.concatenate([z2, up1[n - few :], down1[:few]], axis=0), "z", 1)
    left_2, left_3 = shift(left, "x", 2), shift(left, "x", 3)
    z3, left_2, left_3, down2, up2 = event(z3, left_2, left_3, down2, up2)

    up3 = shift(jnp.concatenate([z3[:n], up2[:half]], axis=0), "y", 1)
    down3 = shift(jnp.concatenate([z3[:n], down2[half - few : n - few]], axis=0), "y", -1)
    row = n - few
    far3 = shift(jnp.concatenate([up2[row + half :], down2[row + half :]], axis=0), "z", 3)
    left, left_last = arrange_left(place, [left, left_1, left_2, left_3])

    def slot(block, up, down, at):
        return [(block, 0, n), (up, 0, n), (down, 0, n), (up2, at, half), (down2, at, half)]

    pieces = slot(own, up0, down0, row + half) + slot(z1, up1, down1, row)
    pieces += [(z2, 0, n), (up2, 0, row), (z3, n, few), (z3, n + few, few), (down2, 0, row), (z3, 0, n)]
    total = multiply_part(left, pieces, "multiply_0")
    far3, down3, up3, total = event(far3, down3, up3, total)

    cut = columns // 2
    lasts = [up3, down3, far3]
    ranges = [(0, n, half), (1, n, half), (0, 0, n), (1, 0, n), (2, 0, n)]
    cuts = (cut, columns - cut)
    sends = multiply_last(token, left_last, total, lasts, ranges, False, cuts, "multiply_1")
    got_0, got_1 = [shift(send, "c", 1) for send in sends]
    (keep,) = multiply_last(token, left_last, total, lasts, ranges, True, (columns,), "multiply_2")
    outs = put(token, keep, [], 0, 0, columns)
    got_0, *outs = event(got_0, *outs)
    outs = put(token, got_0, outs, 1, 0, columns)
    got_1, *outs = event(got_1, *outs)
    return tuple(put(token, got_1, outs, 1, cut, columns))


def solution(mesh):
    fine = Mesh(mesh.devices.reshape(Y, Z, C, H, X), ("y", "z", "c", "h", "x"))
    pop, tp = ("y", "z", "c"), ("h", "x")
    in_specs = (
        P(pop + tp, None, None),
        P(pop + tp, None, None),
        P(pop, None, tp),
        P(pop, None, tp),
        P(pop + tp),
        P(pop + tp),
    )
    out_specs = (P(pop, tp), P(pop, tp))
    return jax.shard_map(shards, mesh=fine, in_specs=in_specs, out_specs=out_specs, check_vma=False)
```

```python
import functools
import math

import jax
import jax.numpy as jnp
from jax import lax
from jax.experimental import pallas as pl
from jax.experimental.pallas import tpu as pltpu
from jax.sharding import Mesh, PartitionSpec as P

Y, Z, C, H, X = 4, 4, 2, 2, 4
ORDER = (
    ((0, 0), (0, 1), (0, 3), (0, 2)),
    ((1, 0), (1, 1), (1, 3), (1, 2)),
    ((2, 0), (2, 1), (2, 3), (3, 0)),
    ((2, 2), (3, 1), (3, 3), (3, 2)),
)


def shift(x, axis, by):
    n = lax.axis_size(axis)
    return lax.ppermute(x, axis, [(i, (i + by) % n) for i in range(n)])


def left_kernel(place_ref, *refs):
    *left_refs, out_ref, last_ref, held = refs
    x, y, z = place_ref[0], place_ref[1], place_ref[2]
    for r, left_ref in enumerate(left_refs):
        held[r] = left_ref[...].astype(held.dtype)
    for k, order in enumerate(ORDER):
        parts = []
        for d, from_y in order:
            chip = lax.rem(y + Y - from_y, Y) * Z + lax.rem(z + Z - d, Z)
            for at_h in range(H):
                for at_x in range(X):
                    parts.append(held[lax.rem(x + X - at_x, X), at_h * Y * Z + chip])
        block = jnp.concatenate(parts, axis=0).T.astype(out_ref.dtype)
        if k < len(ORDER) - 1:
            out_ref[:, k * block.shape[1] : (k + 1) * block.shape[1]] = block
        else:
            last_ref[...] = block


def arrange_left(place, lefts):
    rows = lefts[0].shape[-1]
    size = H * X * lefts[0].shape[1]
    vmem = pl.BlockSpec(memory_space=pltpu.VMEM)
    return pl.pallas_call(
        left_kernel,
        out_shape=(
            jax.ShapeDtypeStruct((rows, (Z - 1) * Y * size), lefts[0].dtype),
            jax.ShapeDtypeStruct((rows, Y * size), lefts[0].dtype),
        ),
        in_specs=[pl.BlockSpec(memory_space=pltpu.SMEM)] + [vmem] * X,
        out_specs=(vmem, vmem),
        scratch_shapes=[pltpu.VMEM((X,) + lefts[0].shape, jnp.float32)],
        compiler_params=pltpu.CompilerParams(vmem_limit_bytes=8 << 20),
        cost_estimate=pl.CostEstimate(flops=0, bytes_accessed=6 << 20, transcendentals=0),
        name="arrange_left",
    )(place, *lefts)


def part_kernel(ranges, width, left_ref, *refs):
    *arrays, out_ref = refs
    left = left_ref[...]
    for at in range(0, out_ref.shape[1], width):
        columns = slice(at, at + width)
        right = jnp.concatenate([arrays[which][row : row + count, columns] for which, row, count in ranges], axis=0)
        out_ref[:, columns] = jnp.dot(left, right, preferred_element_type=jnp.float32)


def multiply_part(left, pieces, name):
    arrays, ranges = [], []
    for array, row, count in pieces:
        known = [k for k, other in enumerate(arrays) if other is array]
        if not known:
            arrays.append(array)
        ranges.append((known[0] if known else len(arrays) - 1, row, count))
    rows, depth = left.shape
    columns = arrays[0].shape[1]
    vmem = pl.BlockSpec(memory_space=pltpu.VMEM)
    return pl.pallas_call(
        functools.partial(part_kernel, ranges, 256),
        out_shape=jax.ShapeDtypeStruct((rows, columns), jnp.float32),
        in_specs=[vmem] * (1 + len(arrays)),
        out_specs=vmem,
        compiler_params=pltpu.CompilerParams(vmem_limit_bytes=24 << 20),
        cost_estimate=pl.CostEstimate(
            flops=2 * rows * columns * depth, bytes_accessed=1 << 20, transcendentals=0
        ),
        name=name,
    )(left, *arrays)


def last_kernel(mine, ranges, width, core_ref, left_ref, total_ref, *refs):
    right_refs, out_refs = refs[:3], refs[3:]
    rows = out_refs[0].shape[0]
    core = core_ref[0] if mine else 1 - core_ref[0]
    row = pl.ds(pl.multiple_of(core * rows, rows), rows)
    start = 0
    for out_ref in out_refs:
        for at in range(0, out_ref.shape[1], width):
            from_at = slice(start + at, start + at + width)
            right = jnp.concatenate([right_refs[k][first : first + count, from_at] for k, first, count in ranges], axis=0)
            total = total_ref[row, from_at]
            total += jnp.dot(left_ref[row], right, preferred_element_type=jnp.float32)
            out_ref[:, at : at + width] = total.astype(out_ref.dtype)
        start += out_ref.shape[1]


def multiply_last(core, left, total, arrays, ranges, mine, cuts, name):
    rows = total.shape[0] // 2
    vmem = pl.BlockSpec(memory_space=pltpu.VMEM)
    return pl.pallas_call(
        functools.partial(last_kernel, mine, ranges, 256),
        out_shape=tuple(jax.ShapeDtypeStruct((rows, cut), left.dtype) for cut in cuts),
        in_specs=[pl.BlockSpec(memory_space=pltpu.SMEM)] + [vmem] * (2 + len(arrays)),
        out_specs=(vmem,) * len(cuts),
        compiler_params=pltpu.CompilerParams(vmem_limit_bytes=14 << 20),
        cost_estimate=pl.CostEstimate(flops=1024 * rows * sum(cuts), bytes_accessed=6 << 20, transcendentals=0),
        name=name,
    )(core, left, total, *arrays)


def put_kernel(got, at, core_ref, part_ref, *refs):
    gate_ref, up_ref, sem = refs[-3:]

    def put(out_ref):
        copy = pltpu.make_async_copy(part_ref, out_ref.at[:, pl.ds(at, part_ref.shape[1])], sem)
        copy.start()
        copy.wait()

    @pl.when(core_ref[0] == got)
    def _():
        put(gate_ref)

    @pl.when(core_ref[0] == 1 - got)
    def _():
        put(up_ref)


def put(core, part, outs, got, at, columns):
    shape = jax.ShapeDtypeStruct((part.shape[0], columns), part.dtype)
    anywhere = pl.BlockSpec(memory_space=pl.ANY)
    return pl.pallas_call(
        functools.partial(put_kernel, got, at),
        out_shape=(shape, shape),
        in_specs=[pl.BlockSpec(memory_space=pltpu.SMEM)] + [anywhere] * (1 + len(outs)),
        out_specs=(anywhere, anywhere),
        scratch_shapes=[pltpu.SemaphoreType.DMA],
        input_output_aliases={2 + k: k for k in range(len(outs))},
        compiler_params=pltpu.CompilerParams(vmem_limit_bytes=4 << 20),
        cost_estimate=pl.CostEstimate(flops=0, bytes_accessed=4 << 20, transcendentals=0),
        name=f"put_{got}_{at}",
    )(core, part, *outs)


def weigh(left, coef):
    return (coef[:, None, None] * left.astype(jnp.float32)).astype(jnp.bfloat16)


def shards(gate_left, up_left, gate_right, up_right, fitness_order, member_scale):
    y, z, core = lax.axis_index("y"), lax.axis_index("z"), lax.axis_index("c")
    first = core == 0
    place = jnp.stack([lax.axis_index("x"), y, z]).astype(jnp.int32)
    token = core.reshape(1).astype(jnp.int32)
    total = Y * Z * C * H * X
    rank, columns = gate_right.shape[1:]

    def event(*arrived):
        nonlocal token
        *arrived, token = lax.optimization_barrier((*arrived, token))
        return arrived

    gate_got, up_got = shift(gate_right, "c", 1), shift(up_right, "c", 1)
    centered = (2 * fitness_order - (total - 1)).astype(jnp.float32)
    coef = centered * member_scale / ((total - 1) * math.sqrt(total * rank))
    gate_w, up_w = weigh(gate_left, coef)[0], weigh(up_left, coef)[0]
    left_mine, left_send = jnp.where(first, gate_w, up_w), jnp.where(first, up_w, gate_w)
    gate_got, up_got, left_mine, left_send, place = event(gate_got, up_got, left_mine, left_send, place)
    own = jnp.concatenate([jnp.where(first, gate_right, up_got), jnp.where(first, gate_got, up_right)], axis=1)
    own = own.reshape(-1, columns)
    left_got = shift(left_send, "c", 1)
    left = jnp.concatenate([jnp.where(first, left_mine, left_got), jnp.where(first, left_got, left_mine)], axis=0)

    def deal(block, axis, at, size):
        width = block.shape[-1] // size
        parts = []
        for by in range(size):
            start = lax.rem(at + by, size) * width
            part = lax.dynamic_slice_in_dim(block, start, width, axis=block.ndim - 1)
            parts.append(shift(part, axis, by) if by else part)
        return parts

    n = own.shape[0]
    half = n // 2

    def both(block):
        return shift(block, "y", 1), shift(block, "y", -1)

    left = left.reshape(C * rank, Y * Z, -1).transpose(1, 0, 2)
    left = jnp.concatenate([left, left], axis=0)
    left = lax.all_to_all(left, ("h", "y", "z"), split_axis=0, concat_axis=0, tiled=True)
    own, = event(own)
    up0, down0 = both(own)
    z1 = shift(own, "z", 1)
    z1, down0, up0 = event(z1, down0, up0)

    up1, down1 = both(z1)
    z2 = shift(z1, "z", 1)
    left, = event(left)
    left_1 = shift(left, "x", 1)
    z2, left, left_1, down1, up1 = event(z2, left, left_1, down1, up1)

    few = n // 4
    up2 = shift(jnp.concatenate([z2[: n - few], up1[:half], up0[:half]], axis=0), "y", 1)
    down2 = shift(jnp.concatenate([z2[few:], down1[half:], down0[half:]], axis=0), "y", -1)
    z3 = shift(jnp.concatenate([z2, up1[n - few :], down1[:few]], axis=0), "z", 1)
    left_2, left_3 = shift(left, "x", 2), shift(left, "x", 3)
    z3, left_2, left_3, up2, down2 = event(z3, left_2, left_3, up2, down2)

    up3 = shift(jnp.concatenate([z3[:n], up2[:half]], axis=0), "y", 1)
    down3 = shift(jnp.concatenate([z3[:n], down2[half - few : n - few]], axis=0), "y", -1)
    row = n - few
    far3 = shift(jnp.concatenate([up2[row + half :], down2[row + half :]], axis=0), "z", 3)
    left, left_last = arrange_left(place, [left, left_1, left_2, left_3])

    def slot(block, up, down, at):
        return [(block, 0, n), (up, 0, n), (down, 0, n), (up2, at, half), (down2, at, half)]

    pieces = slot(own, up0, down0, row + half) + slot(z1, up1, down1, row)
    pieces += [(z2, 0, n), (up2, 0, row), (z3, n, few), (z3, n + few, few), (down2, 0, row), (z3, 0, n)]
    total = multiply_part(left, pieces, "multiply_0")
    far3, down3, up3, total = event(far3, down3, up3, total)

    cut = columns // 1792 * 1280
    lasts = [up3, down3, far3]
    ranges = [(0, n, half), (1, n, half), (0, 0, n), (1, 0, n), (2, 0, n)]
    cuts = (cut, columns - cut)
    sends = multiply_last(token, left_last, total, lasts, ranges, False, cuts, "multiply_1")
    got_0, got_1 = [shift(send, "c", 1) for send in sends]
    (keep,) = multiply_last(token, left_last, total, lasts, ranges, True, (columns,), "multiply_2")
    outs = put(token, keep, [], 0, 0, columns)
    got_0, *outs = event(got_0, *outs)
    outs = put(token, got_0, outs, 1, 0, columns)
    got_1, *outs = event(got_1, *outs)
    return tuple(put(token, got_1, outs, 1, cut, columns))


def solution(mesh):
    fine = Mesh(mesh.devices.reshape(Y, Z, C, H, X), ("y", "z", "c", "h", "x"))
    pop, tp = ("y", "z", "c"), ("h", "x")
    in_specs = (
        P(pop + tp, None, None),
        P(pop + tp, None, None),
        P(pop, None, tp),
        P(pop, None, tp),
        P(pop + tp),
        P(pop + tp),
    )
    out_specs = (P(pop, tp), P(pop, tp))
    return jax.shard_map(shards, mesh=fine, in_specs=in_specs, out_specs=out_specs, check_vma=False)
```
